128 devices in a mesh: blk: 16 (over x, y_hi, core), sub: 8 (over z, y_lo).
Axes of the slice: x: 4, y: 4 (y_hi: 2, y_lo: 2; y = y_hi * 2 + y_lo), z: 4, core: 2. Of those that a mesh axis runs over, the one named last changes fastest.
Arguments:
- left_emb: float32 [2, 200, 65536], P(None, None, ('blk', 'sub')), may hold values from -1.8 to 1.8
- left_state: float32 [65536], P(('blk', 'sub')), may hold values from 0.003 to 0.1
- right_emb: float32 [2, 200, 65536], P(None, None, ('blk', 'sub')), may hold values from -1.8 to 1.8
- right_state: float32 [65536], P(('blk', 'sub')), may hold values from 0.003 to 0.1
- relation_emb: float32 [2, 200, 1280], replicated, may hold values from -4.2 to 4.2
- relation_state: float32 [1280], replicated, may hold values from 0.003 to 0.1
- hub_emb: float32 [2, 200, 4096], replicated, may hold values from -1.8 to 1.8
- hub_state: float32 [4096], replicated, may hold values from 0.003 to 0.1
- heads: int32 [2, 65536], P(None, ('blk', 'sub')), may hold values from 0 to 511
- relations: int32 [2, 65536], P(None, ('blk', 'sub')), may hold values from 0 to 1279
- tails: int32 [2, 65536], P(None, ('blk', 'sub')), may hold values from 0 to 511
- negatives: int32 [2, 131072], P(None, ('blk', 'sub')), may hold values from 0 to 511
- hub_ids: int32 [2, 32768], P(None, ('blk', 'sub')), may hold values from 0 to 4095
Outputs:
- left_out: float32 [2, 200, 65536], P(None, None, ('blk', 'sub'))
- right_out: float32 [2, 200, 65536], P(None, None, ('blk', 'sub'))
- relation_out: float32 [2, 200, 1280], replicated
- hub_out: float32 [2, 200, 4096], replicated
The draws below stay inside these ranges and needn't reach their ends.
Inputs may be any that keep to these rules, and one draw needn't show every extreme that they name: `heads`: local row indices of the head-side block. `relations`: relation types. `tails`: local row indices of the tail-side block held in that bucket. `negatives`: local row indices of the tail-side block held in that bucket; indices may repeat. `hub_ids`: hub rows; indices may repeat.
All inputs are finite; a program needn't handle non-finite values.
Results may differ from the reference program's by a relative error of at most 0.0001.
Values sent between devices are 32-bit elements; how exact they have to be, the bound alone decides.
A program may use at most 128 MiB of HBM per device.

```python
import math
import jax
import jax.numpy as jnp
import numpy as np
from jax import lax

CDIM = 200
NREL = 1280
ROWS = 512
EDGES = 512
NEG = 1024
HUB = 4096
HUB_NEG = 256
BUCKETS = 2
ENTITIES = 65536
ALL_EDGES = 65536
ALL_NEG = 131072
ALL_HUB_NEG = 32768
N_BLK = 16
N_SUB = 8


def set_ends(drawn, rng, smallest, high):
    longest = drawn.shape.index(max(drawn.shape))
    spots = []
    for shift in (0, 1):
        where = [jax.random.randint(jax.random.fold_in(rng, axis), (), 0, length) for axis, length in enumerate(drawn.shape)]
        where[longest] = (where[longest] + shift) % drawn.shape[longest]
        spots.append(tuple(where))
    return drawn.at[spots[0]].set(smallest).at[spots[1]].set(high)


def level_of(stream_key, dims, split, low, top_value):
    loudness, own = 1.0, jax.random.fold_in(stream_key, 6)
    for axis_at, parts in split:
        steps = jnp.exp(jax.random.uniform(jax.random.fold_in(own, axis_at), (parts,), jnp.float32, low / len(split), top_value / len(split)))
        loudness = loudness * jnp.repeat(steps, dims[axis_at] // parts).reshape([-1 if axis == axis_at else 1 for axis in range(len(dims))])
    return loudness


def rank_bounds(amount, slope):
    portions = [(1 << 20) // math.isqrt(standing ** slope) + 1 for standing in range(1, amount + 1)]
    deviation = 1 + sum(portions) // (1 << 30)
    return np.cumsum(np.array([max(1, weight // deviation) for weight in portions]))


def ranked_ids(own_key, dims, amount, slope):
    table = rank_bounds(amount, slope)
    lot = jax.random.randint(jax.random.fold_in(own_key, 1), dims, 0, int(table[amount - 1]))
    standing = jnp.searchsorted(jnp.asarray(table, jnp.int32), lot, side="right")
    return jax.random.permutation(jax.random.fold_in(own_key, 2), amount)[standing].astype(jnp.int32)


def normal_values(own_key, extent, deviation, most, pieces=(), dtype=jnp.bfloat16):
    drawn = deviation * jax.random.normal(own_key, extent, jnp.float32)
    if pieces:
        drawn = drawn * level_of(own_key, extent, pieces, -0.22, 0.18)
    return jnp.clip(drawn, -most, most).astype(dtype)


def setup_inputs(seed: int = 0) -> dict:
    keys = jax.random.split(jax.random.key(seed), 14)
    left_emb = normal_values(keys[0], (2, CDIM, ENTITIES), 0.3, 1.8, ((2, 128),), jnp.float32)
    left_state = jnp.clip(jnp.exp(math.log(0.1) - 3.506558 * jax.random.uniform(keys[1], (ENTITIES,), jnp.float32) ** level_of(keys[1], (ENTITIES,), ((0, 128),), -0.2, 0.2)), 0.003, 0.1)
    right_emb = normal_values(keys[2], (2, CDIM, ENTITIES), 0.3, 1.8, ((2, 128),), jnp.float32)
    right_state = jnp.clip(jnp.exp(math.log(0.1) - 3.506558 * jax.random.uniform(keys[3], (ENTITIES,), jnp.float32) ** level_of(keys[3], (ENTITIES,), ((0, 128),), -0.2, 0.2)), 0.003, 0.1)
    relation_emb = normal_values(keys[4], (2, CDIM, NREL), 0.7, 4.2, (), jnp.float32)
    relation_state = jnp.clip(jnp.exp(jax.random.uniform(keys[5], (NREL,), jnp.float32, math.log(0.003), math.log(0.1))), 0.003, 0.1)
    hub_emb = normal_values(keys[6], (2, CDIM, HUB), 0.3, 1.8, (), jnp.float32)
    hub_state = jnp.clip(jnp.exp(jax.random.uniform(keys[7], (HUB,), jnp.float32, math.log(0.003), math.log(0.1))), 0.003, 0.1)
    heads = set_ends(jax.random.randint(keys[8], (BUCKETS, ALL_EDGES), 0, ROWS), jax.random.fold_in(keys[8], 1), 0, ROWS - 1).astype(jnp.int32)
    relations = set_ends(ranked_ids(keys[9], (BUCKETS, ALL_EDGES), NREL, 2), jax.random.fold_in(keys[9], 3), 0, NREL - 1).astype(jnp.int32)
    tails = set_ends(jax.random.randint(keys[10], (BUCKETS, ALL_EDGES), 0, ROWS), jax.random.fold_in(keys[10], 1), 0, ROWS - 1).astype(jnp.int32)
    negatives = set_ends(jax.random.randint(keys[11], (BUCKETS, ALL_NEG), 0, ROWS), jax.random.fold_in(keys[11], 1), 0, ROWS - 1).astype(jnp.int32)
    hub_ids = set_ends(jax.random.randint(keys[12], (BUCKETS, ALL_HUB_NEG), 0, HUB), jax.random.fold_in(keys[12], 1), 0, HUB - 1).astype(jnp.int32)
    return dict(left_emb=left_emb, left_state=left_state, right_emb=right_emb, right_state=right_state, relation_emb=relation_emb, relation_state=relation_state, hub_emb=hub_emb, hub_state=hub_state, heads=heads, relations=relations, tails=tails, negatives=negatives, hub_ids=hub_ids)


step_rate = 0.25
exact = lax.Precision.HIGHEST

def adagrad(table, state, grads):
    new_state = state + lax.optimization_barrier(jnp.mean(grads * grads, axis=(-3, -2)))
    return (table - step_rate * grads / jnp.sqrt(new_state)[..., None, None, :], new_state)

def bucket_grads(left_block, right_block, relation_emb, hub_emb, head_idx, rel_idx, tail_idx, neg_idx, hub_idx):
    head_rows = left_block[:, :, head_idx]
    rel_rows = relation_emb[:, :, rel_idx]
    tail_rows = right_block[:, :, tail_idx]
    neg_rows = right_block[:, :, neg_idx]
    hub_rows = hub_emb[:, :, hub_idx]
    queries = jnp.stack([head_rows[0] * rel_rows[0] - head_rows[1] * rel_rows[1], head_rows[0] * rel_rows[1] + head_rows[1] * rel_rows[0]])
    positive = lax.optimization_barrier(jnp.sum(queries * tail_rows, axis=(0, 1)))
    neg_scores = jnp.einsum('khe,khn->en', queries, neg_rows, precision=exact)
    hub_scores = jnp.einsum('khe,khn->en', queries, hub_rows, precision=exact)
    weight = 1.0 / (neg_idx.shape[0] + hub_idx.shape[0])
    coef_pos = jax.nn.sigmoid(positive) - 1.0
    coef_neg = jax.nn.sigmoid(neg_scores) * weight
    coef_hub = jax.nn.sigmoid(hub_scores) * weight
    grad_query = coef_pos * tail_rows + jnp.einsum('en,khn->khe', coef_neg, neg_rows, precision=exact) + jnp.einsum('en,khn->khe', coef_hub, hub_rows, precision=exact)
    grad_tail = coef_pos * queries
    grad_neg = jnp.einsum('en,khe->khn', coef_neg, queries, precision=exact)
    grad_hub = jnp.einsum('en,khe->khn', coef_hub, queries, precision=exact)
    grad_head = jnp.stack([grad_query[0] * rel_rows[0] + grad_query[1] * rel_rows[1], grad_query[1] * rel_rows[0] - grad_query[0] * rel_rows[1]])
    grad_rel = jnp.stack([grad_query[0] * head_rows[0] + grad_query[1] * head_rows[1], grad_query[1] * head_rows[0] - grad_query[0] * head_rows[1]])
    left_grad = jnp.zeros_like(left_block).at[:, :, head_idx].add(grad_head)
    right_grad = jnp.zeros_like(right_block).at[:, :, tail_idx].add(grad_tail).at[:, :, neg_idx].add(grad_neg)
    rel_grad = jnp.zeros_like(relation_emb).at[:, :, rel_idx].add(grad_rel)
    hub_grad = jnp.zeros_like(hub_emb).at[:, :, hub_idx].add(grad_hub)
    return (left_grad, right_grad, rel_grad, hub_grad)

def reference(left_emb, left_state, right_emb, right_state, relation_emb, relation_state, hub_emb, hub_state, heads, relations, tails, negatives, hub_ids):
    blocks = N_BLK * N_SUB

    def split_table(table):
        return table.reshape(2, CDIM, blocks, ROWS).transpose(2, 0, 1, 3)

    def join_table(table):
        return table.transpose(1, 2, 0, 3).reshape(2, CDIM, blocks * ROWS)
    left_table = split_table(left_emb)
    right_table = split_table(right_emb)
    left_sums = left_state.reshape(blocks, ROWS)
    right_sums = right_state.reshape(blocks, ROWS)
    rel_total = jnp.zeros_like(relation_emb)
    hub_total = jnp.zeros_like(hub_emb)
    per_block = jax.vmap(bucket_grads, in_axes=(0, 0, None, None, 0, 0, 0, 0, 0))
    for bucket in range(BUCKETS):
        left_grad, right_grad, rel_grad, hub_grad = per_block(left_table, right_table, relation_emb, hub_emb, heads[bucket].reshape(blocks, EDGES), relations[bucket].reshape(blocks, EDGES), tails[bucket].reshape(blocks, EDGES), negatives[bucket].reshape(blocks, NEG), hub_ids[bucket].reshape(blocks, HUB_NEG))
        left_table, left_sums = adagrad(left_table, left_sums, left_grad)
        right_table, right_sums = adagrad(right_table, right_sums, right_grad)
        rel_total = rel_total + lax.optimization_barrier(jnp.sum(rel_grad, axis=0))
        hub_total = hub_total + lax.optimization_barrier(jnp.sum(hub_grad, axis=0))
        if bucket < BUCKETS - 1:
            right_table = jnp.roll(right_table.reshape(N_BLK, N_SUB, 2, CDIM, ROWS), 1, axis=0).reshape(blocks, 2, CDIM, ROWS)
            right_sums = jnp.roll(right_sums.reshape(N_BLK, N_SUB, ROWS), 1, axis=0).reshape(blocks, ROWS)
    relation_out, unused_rel = adagrad(relation_emb, relation_state, rel_total)
    hub_out, unused_hub = adagrad(hub_emb, hub_state, hub_total)
    return (join_table(left_table), join_table(right_table), relation_out, hub_out)
```

```python
import functools
import jax
import jax.numpy as jnp
from jax import lax
from jax.experimental import pallas as pl
from jax.experimental.pallas import tpu as pltpu
from jax.sharding import PartitionSpec as P

RATE = 0.25
F32, BF16 = jnp.float32, jnp.bfloat16
NN = (((1,), (0,)), ((), ()))
NT = (((1,), (1,)), ((), ()))


def mm(a, b, dims=NN):
    return lax.dot_general(a, b, dims, preferred_element_type=F32)


def halves(x):
    hi = x.astype(BF16)
    return hi, (x - hi.astype(F32)).astype(BF16)


def stacked(x):
    hi, lo = halves(x)
    return jnp.concatenate([hi, lo], axis=0)


def mm3(a2, b_hi, b_lo, dims=NN):
    n = a2.shape[0] // 2
    both = mm(a2, b_hi, dims)
    return both[:n] + both[n:] + mm(a2[:n], b_lo, dims)


def fold(x):
    n = x.shape[0] // 2
    return x[:n] + x[n:]


def rows_hot(idx, base, count):
    at = lax.broadcasted_iota(jnp.int32, (count, idx.shape[1]), 0) + base
    return (at == idx).astype(F32).astype(BF16)


def column(idx):
    parts = []
    for k in range(0, idx.shape[1], 128):
        parts.append(jnp.broadcast_to(idx[:, k : k + 128], (128, 128)).T)
    return jnp.concatenate(parts, axis=0)


def lanes_hot(col, base, count):
    at = lax.broadcasted_iota(jnp.int32, (col.shape[0], 128), 1)
    return jnp.concatenate([col == at + (base + k) for k in range(0, count, 128)], axis=1)


def adagrad(table, state, grad):
    new_state = state + jnp.sum(grad * grad, axis=0, keepdims=True) * (1.0 / grad.shape[0])
    return table - grad * (RATE / jnp.sqrt(new_state)), new_state


def sigmoid(x):
    return 1.0 / (1.0 + jnp.exp(-x))


def cmul(a, b):
    n = a.shape[0] // 2
    a0, a1, b0, b1 = a[:n], a[n:], b[:n], b[n:]
    return jnp.concatenate([a0 * b0 - a1 * b1, a0 * b1 + a1 * b0], axis=0)


def cmul_conj(a, b):
    n = a.shape[0] // 2
    a0, a1, b0, b1 = a[:n], a[n:], b[:n], b[n:]
    return jnp.concatenate([a0 * b0 + a1 * b1, a1 * b0 - a0 * b1], axis=0)


def gather_loop(table_ref, idx, out_ref, block):
    count = table_ref.shape[1]
    out_ref[...] = jnp.zeros_like(out_ref)

    @pl.loop(0, count // block)
    def _(k):
        base = pl.multiple_of(k * block, block)
        out_ref[...] += mm(stacked(table_ref[:, pl.ds(base, block)]), rows_hot(idx, base, block))


def gather(table, idx):
    return mm(stacked(table), rows_hot(idx, 0, table.shape[1]))


def queries_side(q):
    qt = q.T
    return stacked(qt)


def first(bucket_weight, left_ref, lstate_ref, right_ref, rstate_ref, rel_ref, hub_ref, heads_ref, rels_ref,
          tails_ref, negs_ref, hubs_ref, left_out, lstate_out, right_out, rstate_out, h1_out, r1_out, q1_out,
          dqh1_out, dr0_out, ghub_out, u_ref, r_ref, du_ref):
    w = bucket_weight
    rows = left_ref.shape[1]
    e = heads_ref.shape[1]
    left = left_ref[...]
    right = right_ref[...]
    idx_r = jnp.concatenate([rels_ref[0:1, :], rels_ref[1:2, :]], axis=1)
    gather_loop(rel_ref, idx_r, r_ref, 256)
    h0 = fold(gather(left, heads_ref[0:1, :]))
    r0 = fold(r_ref[:, :e])
    q0 = cmul(h0, r0)
    q0t = stacked(q0.T)
    rh, rl = halves(right)
    coef = coefs(mm3(q0t, rh, rl), w, tails_ref[0:1, :], negs_ref[0:1, :], rows)
    ch, cl = halves(coef)
    q02 = stacked(q0)
    g = mm3(q02, ch, cl)
    right_out[...], rstate_out[...] = adagrad(right, rstate_ref[...], g)
    idx_u = jnp.concatenate([hubs_ref[0:1, :], hubs_ref[1:2, :]], axis=1)
    gather_loop(hub_ref, idx_u, u_ref, 512)
    m = hubs_ref.shape[1]
    u0h, u0l = u_ref[:400, :m].astype(BF16), u_ref[400:, :m].astype(BF16)
    ch2, cl2 = halves(sigmoid(mm3(q0t, u0h, u0l)) * w)
    du_ref[:, :m] = mm3(q02, ch2, cl2)
    r2 = jnp.concatenate([rh, rl], axis=0)
    u2 = jnp.concatenate([u0h, u0l], axis=0)
    dq = mm3(r2, ch, cl, NT) + mm3(u2, ch2, cl2, NT)
    dh = cmul_conj(dq, r0)
    dr0_out[...] = cmul_conj(dq, h0)
    gl = fold(mm(stacked(dh), lanes_hot(column(heads_ref[0:1, :]), 0, rows).astype(F32).astype(BF16)))
    left1, lstate_out[...] = adagrad(left, lstate_ref[...], gl)
    left_out[...] = left1
    h1 = fold(gather(left1, heads_ref[1:2, :]))
    r1 = fold(r_ref[:, e:])
    q1 = cmul(h1, r1)
    h1_out[...] = h1
    r1_out[...] = r1
    q1_out[...] = q1
    q1t = stacked(q1.T)
    u1h, u1l = u_ref[:400, m:].astype(BF16), u_ref[400:, m:].astype(BF16)
    ch3, cl3 = halves(sigmoid(mm3(q1t, u1h, u1l)) * w)
    du_ref[:, m:] = mm3(stacked(q1), ch3, cl3)
    dqh1_out[...] = mm3(jnp.concatenate([u1h, u1l], axis=0), ch3, cl3, NT)
    scatter_loop(du_ref[...], column(idx_u), ghub_out, 512)


def scatter_loop(grad, col, out_ref, block):
    g2 = stacked(grad)

    @pl.loop(0, out_ref.shape[1] // block)
    def _(k):
        base = pl.multiple_of(k * block, block)
        hot = lanes_hot(col, base, block).astype(F32).astype(BF16)
        out_ref[:, pl.ds(base, block)] = fold(mm(g2, hot))


def coefs(score, w, tail_idx, neg_idx, rows):
    times = jnp.sum(rows_hot_f(neg_idx, rows), axis=1, keepdims=True)
    times = jnp.broadcast_to(times, (rows, 128)).T[0:1, :] * w
    tail = lanes_hot(column(tail_idx), 0, rows)
    s = sigmoid(score)
    return s * times + jnp.where(tail, s - 1.0, 0.0)


def rows_hot_f(idx, count):
    at = lax.broadcasted_iota(jnp.int32, (count, idx.shape[1]), 0)
    return (at == idx).astype(F32)


def second(bucket_weight, left_ref, lstate_ref, right_ref, rstate_ref, h1_ref, r1_ref, q1_ref, dqh1_ref, dr0_ref,
           heads_ref, rels_ref, tails_ref, negs_ref, left_out, right_out, grel_out):
    w = bucket_weight
    right = right_ref[...]
    rows = right.shape[1]
    q1 = q1_ref[...]
    rh, rl = halves(right)
    coef = coefs(mm3(stacked(q1.T), rh, rl), w, tails_ref[1:2, :], negs_ref[1:2, :], rows)
    ch, cl = halves(coef)
    dq = mm3(jnp.concatenate([rh, rl], axis=0), ch, cl, NT) + dqh1_ref[...]
    dr = jnp.concatenate([dr0_ref[...], cmul_conj(dq, h1_ref[...])], axis=1)
    col_r = column(jnp.concatenate([rels_ref[0:1, :], rels_ref[1:2, :]], axis=1))
    scatter_loop(dr, col_r, grel_out, 256)
    dh = cmul_conj(dq, r1_ref[...])
    g = mm3(stacked(q1), ch, cl)
    right_out[...], _ = adagrad(right, rstate_ref[...], g)
    gl = fold(mm(stacked(dh), lanes_hot(column(heads_ref[1:2, :]), 0, rows).astype(F32).astype(BF16)))
    left_out[...], _ = adagrad(left_ref[...], lstate_ref[...], gl)


def shards(left_emb, left_state, right_emb, right_state, relation_emb, relation_state, hub_emb, hub_state, heads,
           relations, tails, negatives, hub_ids):
    two, half, rows = left_emb.shape
    feats = two * half
    e = heads.shape[1]
    w = 1.0 / (negatives.shape[1] + hub_ids.shape[1])
    left = left_emb.reshape(feats, rows)
    right = right_emb.reshape(feats, rows)
    rel = relation_emb.reshape(feats, -1)
    hub = hub_emb.reshape(feats, -1)
    sd = lambda *s: jax.ShapeDtypeStruct(s, F32)
    vm = pl.BlockSpec(memory_space=pltpu.VMEM)
    params = pltpu.CompilerParams(vmem_limit_bytes=56 * 2**20)
    outs = [sd(feats, rows), sd(1, rows), sd(feats, rows), sd(1, rows), sd(feats, e), sd(feats, e), sd(feats, e),
            sd(feats, e), sd(feats, e), sd(feats, hub.shape[1])]
    left1, ls1, right1, rs1, h1, r1, q1, dqh1, dr0, ghub = pl.pallas_call(
        functools.partial(first, w), out_shape=outs, in_specs=[vm] * 11, out_specs=[vm] * len(outs),
        scratch_shapes=[pltpu.VMEM((2 * feats, 2 * hub_ids.shape[1]), F32), pltpu.VMEM((2 * feats, 2 * e), F32),
                        pltpu.VMEM((feats, 2 * hub_ids.shape[1]), F32)],
        compiler_params=params, name="first_bucket",
    )(left, left_state[None], right, right_state[None], rel, hub, heads, relations, tails, negatives, hub_ids)
    n = lax.axis_size("blk")
    right1, rs1 = lax.ppermute((right1, rs1), "blk", [(i, (i + 1) % n) for i in range(n)])
    outs = [sd(feats, rows), sd(feats, rows), sd(feats, rel.shape[1])]
    left2, right2, grel = pl.pallas_call(
        functools.partial(second, w), out_shape=outs, in_specs=[vm] * 13, out_specs=[vm] * 3,
        compiler_params=params, name="second_bucket",
    )(left1, ls1, right1, rs1, h1, r1, q1, dqh1, dr0, heads, relations, tails, negatives)
    grel, ghub = lax.psum((grel, ghub), ("blk", "sub"))

    def step(table, state, grads):
        new = state + jnp.mean(grads * grads, axis=0)
        return table - RATE * grads / jnp.sqrt(new)[None, :]

    return (left2.reshape(left_emb.shape), right2.reshape(right_emb.shape),
            step(rel, relation_state, grel).reshape(relation_emb.shape),
            step(hub, hub_state, ghub).reshape(hub_emb.shape))


def solution(mesh):
    cut = P(None, None, ("blk", "sub"))
    row = P(("blk", "sub"))
    idx = P(None, ("blk", "sub"))
    return jax.shard_map(shards, mesh=mesh, in_specs=(cut, row, cut, row, P(), P(), P(), P(), idx, idx, idx, idx, idx),
                         out_specs=(cut, cut, P(), P()), check_vma=False)
```

```python
import functools
import jax
import jax.numpy as jnp
from jax import lax
from jax.experimental import pallas as pl
from jax.experimental.pallas import tpu as pltpu
from jax.sharding import PartitionSpec as P

RATE = 0.25
F32, BF16 = jnp.float32, jnp.bfloat16
NN = (((1,), (0,)), ((), ()))
NT = (((1,), (1,)), ((), ()))


def mm(a, b, dims=NN):
    return lax.dot_general(a, b, dims, preferred_element_type=F32)


def halves(x):
    hi = x.astype(BF16)
    return hi, (x - hi.astype(F32)).astype(BF16)


def stacked(x):
    hi, lo = halves(x)
    return jnp.concatenate([hi, lo], axis=0)


def mm3(a2, b_hi, b_lo, dims=NN):
    n = a2.shape[0] // 2
    both = mm(a2, b_hi, dims)
    return both[:n] + both[n:] + mm(a2[:n], b_lo, dims)


def fold(x):
    n = x.shape[0] // 2
    return x[:n] + x[n:]


def rows_hot(idx, base, count):
    at = lax.broadcasted_iota(jnp.int32, (count, idx.shape[1]), 0) + base
    return (at == idx).astype(F32).astype(BF16)


def column(idx):
    parts = []
    for k in range(0, idx.shape[1], 128):
        parts.append(jnp.broadcast_to(idx[:, k : k + 128], (128, 128)).T)
    return jnp.concatenate(parts, axis=0)


def lanes_hot(col, base, count):
    at = lax.broadcasted_iota(jnp.int32, (col.shape[0], 128), 1)
    return jnp.concatenate([col == at + (base + k) for k in range(0, count, 128)], axis=1)


def adagrad(table, state, grad):
    new_state = state + jnp.sum(grad * grad, axis=0, keepdims=True) * (1.0 / grad.shape[0])
    return table - grad * (RATE / jnp.sqrt(new_state)), new_state


def sigmoid(x):
    return 1.0 / (1.0 + jnp.exp(-x))


def cmul(a, b):
    n = a.shape[0] // 2
    a0, a1, b0, b1 = a[:n], a[n:], b[:n], b[n:]
    return jnp.concatenate([a0 * b0 - a1 * b1, a0 * b1 + a1 * b0], axis=0)


def cmul_conj(a, b):
    n = a.shape[0] // 2
    a0, a1, b0, b1 = a[:n], a[n:], b[:n], b[n:]
    return jnp.concatenate([a0 * b0 + a1 * b1, a1 * b0 - a0 * b1], axis=0)


def gather_loop(table_ref, idx, out_ref, block):
    count = table_ref.shape[1]
    out_ref[...] = jnp.zeros_like(out_ref)

    @pl.loop(0, count // block)
    def _(k):
        base = pl.multiple_of(k * block, block)
        out_ref[...] += mm(stacked(table_ref[:, pl.ds(base, block)]), rows_hot(idx, base, block))


def gather(table, idx):
    return mm(stacked(table), rows_hot(idx, 0, table.shape[1]))


def queries_side(q):
    qt = q.T
    return stacked(qt)


def first_right(w, left_ref, right_ref, rstate_ref, rel_ref, heads_ref, rels_ref, tails_ref, negs_ref,
                right_out, rstate_out, h0_out, r_out, q0_out, c_out, r_ref):
    rows = left_ref.shape[1]
    e = heads_ref.shape[1]
    right = right_ref[...]
    idx_r = jnp.concatenate([rels_ref[0:1, :], rels_ref[1:2, :]], axis=1)
    gather_loop(rel_ref, idx_r, r_ref, 256)
    r_out[...] = fold(r_ref[...])
    h0 = fold(gather(left_ref[...], heads_ref[0:1, :]))
    r0 = r_out[:, :e]
    q0 = cmul(h0, r0)
    h0_out[...] = h0
    q0_out[...] = q0
    rh, rl = halves(right)
    coef = coefs(mm3(stacked(q0.T), rh, rl), w, tails_ref[0:1, :], negs_ref[0:1, :], rows)
    c_out[...] = coef
    ch, cl = halves(coef)
    right_out[...], rstate_out[...] = adagrad(right, rstate_ref[...], mm3(stacked(q0), ch, cl))


def first_left(w, left_ref, lstate_ref, right_ref, hub_ref, heads_ref, hubs_ref, h0_ref, r_ref, q0_ref, c_ref,
               left_out, lstate_out, h1_out, q1_out, dqh1_out, dr0_out, du_ref, u_ref):
    rows = left_ref.shape[1]
    feats = left_ref.shape[0]
    e = heads_ref.shape[1]
    left = left_ref[...]
    q0 = q0_ref[...]
    r0 = r_ref[:, :e]
    q0t = stacked(q0.T)
    q02 = stacked(q0)
    idx_u = jnp.concatenate([hubs_ref[0:1, :], hubs_ref[1:2, :]], axis=1)
    gather_loop(hub_ref, idx_u, u_ref, 512)
    m = hubs_ref.shape[1]
    u0h, u0l = u_ref[:feats, :m].astype(BF16), u_ref[feats:, :m].astype(BF16)
    ch2, cl2 = halves(sigmoid(mm3(q0t, u0h, u0l)) * w)
    du_ref[:feats, :m] = mm3(q02, ch2, cl2)
    ch, cl = halves(c_ref[...])
    u2 = jnp.concatenate([u0h, u0l], axis=0)
    dq = mm3(stacked(right_ref[...]), ch, cl, NT) + mm3(u2, ch2, cl2, NT)
    dh = cmul_conj(dq, r0)
    dr0_out[...] = cmul_conj(dq, h0_ref[...])
    gl = fold(mm(stacked(dh), lanes_hot(column(heads_ref[0:1, :]), 0, rows).astype(F32).astype(BF16)))
    left1, lstate_out[...] = adagrad(left, lstate_ref[...], gl)
    left_out[...] = left1
    h1 = fold(gather(left1, heads_ref[1:2, :]))
    q1 = cmul(h1, r_ref[:, e:])
    h1_out[...] = h1
    q1_out[...] = q1
    u1h, u1l = u_ref[:feats, m:].astype(BF16), u_ref[feats:, m:].astype(BF16)
    ch3, cl3 = halves(sigmoid(mm3(stacked(q1.T), u1h, u1l)) * w)
    du_ref[:feats, m:] = mm3(stacked(q1), ch3, cl3)
    dqh1_out[...] = mm3(jnp.concatenate([u1h, u1l], axis=0), ch3, cl3, NT)
    du_ref[feats:, :] = jnp.broadcast_to(idx_u.astype(F32), (8, 2 * m))


def coefs(score, w, tail_idx, neg_idx, rows):
    times = jnp.sum(rows_hot_f(neg_idx, rows), axis=1, keepdims=True)
    times = jnp.broadcast_to(times, (rows, 128)).T[0:1, :] * w
    tail = lanes_hot(column(tail_idx), 0, rows)
    s = sigmoid(score)
    return s * times + jnp.where(tail, s - 1.0, 0.0)


def rows_hot_f(idx, count):
    at = lax.broadcasted_iota(jnp.int32, (count, idx.shape[1]), 0)
    return (at == idx).astype(F32)


HT, RT = 17, 6
MESH = pl.DeviceIdType.MESH


class Place:
    def __init__(self):
        b, s = lax.axis_index("blk"), lax.axis_index("sub")
        self.core = lax.rem(b, 2)
        self.pos = [b // 4, lax.rem(b // 2, 2) * 2 + lax.rem(s, 2), s // 2]

    def at(self, pos, core):
        return ((pos[0] * 2 + pos[1] // 2) * 2 + core, pos[2] * 2 + lax.rem(pos[1], 2))

    def shift(self, axis, d):
        pos = list(self.pos)
        pos[axis] = lax.rem(pos[axis] + d, 4)
        return self.at(pos, self.core)

    def sibling(self):
        return self.at(self.pos, 1 - self.core)


class Reduce:
    def __init__(self, place, n, g, rb1, s1, rb2, s2, rb3, full, sems):
        self.p, self.n = place, n
        self.g, self.rb1, self.s1, self.rb2, self.s2, self.rb3, self.full = g, rb1, s1, rb2, s2, rb3, full
        self.sems = sems
        self.live = {}

    def copy(self, stage, part, k, src, dst, dev):
        return pltpu.make_async_remote_copy(
            src_ref=src, dst_ref=dst, send_sem=self.sems.at[0, stage, part, k], recv_sem=self.sems.at[1, stage, part, k],
            device_id=dev, device_id_type=MESH)

    def put(self, stage, part, k, src, dst, dev):
        c = self.copy(stage, part, k, src, dst, dev)
        c.start()
        self.live[stage, part, k] = c

    def axis(self, part, level):
        return (part + level) % 3

    def here(self, part, level):
        return self.p.pos[self.axis(part, level)]

    def rs1(self, part):
        n, c, a = self.n, self.here(part, 0), self.axis(part, 0)
        for d in (2, 1, 3):
            off = part * 16 * n + lax.rem(c + d, 4) * (4 * n)
            self.put(0, part, d - 1, self.g.at[pl.ds(off, 4 * n)], self.rb1.at[part, d - 1], self.p.shift(a, d))

    def rs1_done(self, part):
        n, c = self.n, self.here(part, 0)
        for d in (1, 3, 2):
            self.live[0, part, d - 1].wait_recv()
        off = part * 16 * n + c * (4 * n)
        self.s1[part] = (self.g[pl.ds(off, 4 * n)] + self.rb1[part, 0]) + (self.rb1[part, 1] + self.rb1[part, 2])

    def rs2(self, part):
        n, c, a = self.n, self.here(part, 1), self.axis(part, 1)
        for d in (2, 1, 3):
            self.put(1, part, d - 1, self.s1.at[part, pl.ds(lax.rem(c + d, 4) * n, n)], self.rb2.at[part, d - 1],
                     self.p.shift(a, d))

    def rs2_done(self, part):
        n, c = self.n, self.here(part, 1)
        for d in (1, 3, 2):
            self.live[1, part, d - 1].wait_recv()
        self.s2[part] = (self.s1[part, pl.ds(c * n, n)] + self.rb2[part, 0]) + (self.rb2[part, 1] + self.rb2[part, 2])

    def ar3(self, part):
        c, a = self.here(part, 2), self.axis(part, 2)
        for d in (2, 1, 3):
            self.put(2, part, d - 1, self.s2.at[part], self.rb3.at[part, c], self.p.shift(a, d))
        self.rb3[part, c] = self.s2[part]

    def mine(self, part):
        n = self.n
        return part * 16 * n + self.here(part, 0) * (4 * n) + self.here(part, 1) * n

    def ar3_done(self, part):
        for d in (1, 3, 2):
            self.live[2, part, d - 1].wait_recv()
        self.full[self.p.core, pl.ds(self.mine(part), self.n)] = (
            (self.rb3[part, 0] + self.rb3[part, 1]) + (self.rb3[part, 2] + self.rb3[part, 3]))

    def ag2(self, part):
        a = self.axis(part, 1)
        ref = self.full.at[self.p.core, pl.ds(self.mine(part), self.n)]
        for d in (2, 1, 3):
            self.put(3, part, d - 1, ref, ref, self.p.shift(a, d))

    def ag2_done(self, part):
        for d in (1, 3, 2):
            self.live[3, part, d - 1].wait_recv()

    def chunk(self, part, c):
        return self.full.at[self.p.core, pl.ds(part * 16 * self.n + c * (4 * self.n), 4 * self.n)]

    def ag1(self, part):
        c, a = self.here(part, 0), self.axis(part, 0)
        ref = self.chunk(part, c)
        for d in (2, 1, 3):
            self.put(4, part, d - 1, ref, ref, self.p.shift(a, d))
        self.put(5, part, 3, ref, ref, self.p.sibling())

    def ag1_done(self, part):
        c = self.here(part, 0)
        for d in (1, 3, 2):
            self.live[4, part, d - 1].wait_recv()
            ref = self.chunk(part, lax.rem(c + 4 - d, 4))
            self.put(5, part, d - 1, ref, ref, self.p.sibling())

    def finish(self, part):
        for k in range(4):
            self.live[5, part, k].wait_recv()
        for c in self.live:
            if c[1] == part:
                self.live[c].wait_send()


def tiles_of(x):
    return [x[:, k : k + 128].reshape(x.shape[0] // 8, 8, 128) for k in range(0, x.shape[1], 128)]


def scatter_into(g_ref, at, grad2, col, base, width, add):
    hot = lanes_hot(col, base, width).astype(F32).astype(BF16)
    for j, t in enumerate(tiles_of(fold(mm(grad2, hot)))):
        n = t.shape[0]
        here = pl.ds(at + j * n, n)
        g_ref[here] = g_ref[here] + t if add else t


def second(w, du_ref, dr0_ref, left_ref, lstate_ref, right_ref, rstate_ref, h1_ref, r_ref, q1_ref, dqh1_ref,
           heads_ref, rels_ref, tails_ref, negs_ref, left_out, right_out, ghub_out, grel_out,
           dus, dro, drs, hg, hrb1, hs1, hrb2, hs2, hrb3, hfull, rg, rrb1, rs1, rrb2, rs2, rrb3, rfull, hsem, rsem,
           xsem, osem):
    place = Place()
    feats, rows = left_ref.shape
    e = q1_ref.shape[1]
    hub = Reduce(place, HT, hg, hrb1, hs1, hrb2, hs2, hrb3, hfull, hsem)
    rel = Reduce(place, RT, rg, rrb1, rs1, rrb2, rs2, rrb3, rfull, rsem)
    barrier = pltpu.get_barrier_semaphore()
    for a in range(3):
        for d in (1, 2, 3):
            pl.semaphore_signal(barrier, inc=1, device_id=place.shift(a, d), device_id_type=MESH)
    pl.semaphore_signal(barrier, inc=1, device_id=place.sibling(), device_id_type=MESH)
    pl.semaphore_wait(barrier, 10)

    def to_sibling(k, src, dst):
        c = pltpu.make_async_remote_copy(src_ref=src, dst_ref=dst, send_sem=xsem.at[0, k], recv_sem=xsem.at[1, k],
                                         device_id=place.sibling(), device_id_type=MESH)
        c.start()
        return c

    x_u = to_sibling(0, du_ref, dus)
    dro[0, :feats, :] = dr0_ref[...]
    dro[0, feats:, :] = jnp.broadcast_to(rels_ref[0:1, :].astype(F32), (8, e))
    x_r0 = to_sibling(1, dro.at[0], drs.at[0])

    hub_lanes = 2048
    first_lane = place.core * hub_lanes
    own2 = stacked(du_ref[:feats, :])
    own_col = column(du_ref[feats : feats + 1, :].astype(jnp.int32))
    for k in range(4):
        scatter_into(hg, k * 200, own2, own_col, first_lane + k * 512, 512, False)
    hg[800:, :, :] = jnp.zeros((48 * HT - 800, 8, 128), F32)
    x_u.wait_recv()
    sib2 = stacked(dus[:feats, :])
    sib_col = column(dus[feats : feats + 1, :].astype(jnp.int32))
    for k in range(4):
        scatter_into(hg, k * 200, sib2, sib_col, first_lane + k * 512, 512, True)
        if k:
            hub.rs1(k - 1)

    right = right_ref[...]
    q1 = q1_ref[...]
    rh, rl = halves(right)
    coef = coefs(mm3(stacked(q1.T), rh, rl), w, tails_ref[1:2, :], negs_ref[1:2, :], rows)
    ch, cl = halves(coef)
    dq = mm3(jnp.concatenate([rh, rl], axis=0), ch, cl, NT) + dqh1_ref[...]
    dro[1, :feats, :] = cmul_conj(dq, h1_ref[...])
    dro[1, feats:, :] = jnp.broadcast_to(rels_ref[1:2, :].astype(F32), (8, e))
    x_r1 = to_sibling(2, dro.at[1], drs.at[1])
    rel_lanes = 640
    first_rel = place.core * rel_lanes
    x_r0.wait_recv()

    def rel_scatter(x, add):
        scatter_into(rg, 0, stacked(x[:feats, :]), column(x[feats : feats + 1, :].astype(jnp.int32)), first_rel, 640,
                     add)

    rel_scatter(dro[0], False)
    rel_scatter(drs[0], True)
    rel_scatter(dro[1], True)
    rg[250:, :, :] = jnp.zeros((48 * RT - 250, 8, 128), F32)
    x_r1.wait_recv()
    rel_scatter(drs[1], True)
    for p in range(3):
        rel.rs1(p)
    for p in range(3):
        hub.rs1_done(p)
        hub.rs2(p)
    g = mm3(stacked(q1), ch, cl)
    right_out[...], _ = adagrad(right, rstate_ref[...], g)
    for p in range(3):
        rel.rs1_done(p)
        rel.rs2(p)
    for p in range(3):
        hub.rs2_done(p)
        hub.ar3(p)
    dh = cmul_conj(dq, r_ref[:, e:])
    gl = fold(mm(stacked(dh), lanes_hot(column(heads_ref[1:2, :]), 0, rows).astype(F32).astype(BF16)))
    left_out[...], _ = adagrad(left_ref[...], lstate_ref[...], gl)
    for p in range(3):
        hub.ar3_done(p)
        hub.ag2(p)
    for p in range(3):
        rel.rs2_done(p)
        rel.ar3(p)
    for p in range(3):
        hub.ag2_done(p)
        hub.ag1(p)
    for p in range(3):
        rel.ar3_done(p)
        rel.ag2(p)
    for p in range(3):
        rel.ag2_done(p)
        rel.ag1(p)
    for p in range(3):
        hub.ag1_done(p)
    for p in range(3):
        rel.ag1_done(p)
    for p in range(3):
        hub.finish(p)
        rel.finish(p)
    x_u.wait_send()
    x_r0.wait_send()
    x_r1.wait_send()
    a = pltpu.make_async_copy(hfull, ghub_out, osem.at[0])
    b = pltpu.make_async_copy(rfull, grel_out, osem.at[1])
    a.start()
    b.start()
    a.wait()
    b.wait()


def update(table_ref, state_ref, g_ref, out_ref):
    for j in range(table_ref.shape[1] // 128):
        lanes = slice(j * 128, (j + 1) * 128)
        n = table_ref.shape[0] // 8
        g = g_ref[0, j * n : (j + 1) * n].reshape(table_ref.shape[0], 128)
        new = state_ref[:, lanes] + jnp.sum(g * g, axis=0, keepdims=True) * (1.0 / table_ref.shape[0])
        out_ref[:, lanes] = table_ref[:, lanes] - g * (RATE / jnp.sqrt(new))


def apply(table, state, g, width, name):
    feats, lanes = table.shape
    per = lanes // 2 // width
    at = lambda h, k: (0, h * per + k)
    return pl.pallas_call(
        update, out_shape=jax.ShapeDtypeStruct(table.shape, F32), grid=(2, per),
        in_specs=[pl.BlockSpec((feats, width), at), pl.BlockSpec((1, width), at),
                  pl.BlockSpec((1, feats // 8 * width // 128, 8, 128), lambda h, k: (h, k, 0, 0))],
        out_specs=pl.BlockSpec((feats, width), at), name=name,
        compiler_params=pltpu.CompilerParams(vmem_limit_bytes=40 * 2**20),
    )(table, state[None], g)


def shards(left_emb, left_state, right_emb, right_state, relation_emb, relation_state, hub_emb, hub_state, heads,
           relations, tails, negatives, hub_ids):
    two, half, rows = left_emb.shape
    feats = two * half
    e = heads.shape[1]
    m = hub_ids.shape[1]
    w = 1.0 / (negatives.shape[1] + hub_ids.shape[1])
    left = left_emb.reshape(feats, rows)
    right = right_emb.reshape(feats, rows)
    rel = relation_emb.reshape(feats, -1)
    hub = hub_emb.reshape(feats, -1)
    sd = lambda *s: jax.ShapeDtypeStruct(s, F32)
    vm = pl.BlockSpec(memory_space=pltpu.VMEM)
    hbm = pl.BlockSpec(memory_space=pl.ANY)
    params = pltpu.CompilerParams(vmem_limit_bytes=50 * 2**20)
    outs = [sd(feats, rows), sd(1, rows), sd(feats, e), sd(feats, 2 * e), sd(feats, e), sd(e, rows)]
    right1, rs1, h0, r, q0, c0 = pl.pallas_call(
        functools.partial(first_right, w), out_shape=outs, in_specs=[vm] * 8, out_specs=[vm] * len(outs),
        scratch_shapes=[pltpu.VMEM((2 * feats, 2 * e), F32)],
        compiler_params=params, name="first_right",
        cost_estimate=pl.CostEstimate(flops=6 * 10**9, bytes_accessed=10**7, transcendentals=0),
    )(left, right, right_state[None], rel, heads, relations, tails, negatives)
    n = lax.axis_size("blk")
    right1, rs1 = lax.ppermute((right1, rs1), "blk", [(i, (i + 1) % n) for i in range(n)])
    outs = [sd(feats, rows), sd(1, rows), sd(feats, e), sd(feats, e), sd(feats, e), sd(feats, e), sd(feats + 8, 2 * m)]
    left1, ls1, h1, q1, dqh1, dr0, du = pl.pallas_call(
        functools.partial(first_left, w), out_shape=outs, in_specs=[vm] * 10, out_specs=[vm] * len(outs),
        scratch_shapes=[pltpu.VMEM((2 * feats, 2 * m), F32)],
        compiler_params=params, name="first_left",
        cost_estimate=pl.CostEstimate(flops=10 * 10**9, bytes_accessed=4 * 10**7, transcendentals=0),
    )(left, left_state[None], right, hub, heads, hub_ids, h0, r, q0, c0)
    tile = lambda *s: pltpu.VMEM((*s, 8, 128), F32)
    stage = lambda n: [tile(48 * n), tile(3, 3, 4 * n), tile(3, 4 * n), tile(3, 3, n), tile(3, n), tile(3, 4, n),
                       tile(2, 48 * n)]
    outs = [sd(feats, rows), sd(feats, rows), sd(2, 48 * HT, 8, 128), sd(2, 48 * RT, 8, 128)]
    left2, right2, ghub, grel = pl.pallas_call(
        functools.partial(second, w), out_shape=outs, in_specs=[vm] * 14, out_specs=[vm, vm, hbm, hbm],
        scratch_shapes=[pltpu.VMEM((feats + 8, 2 * m), F32), pltpu.VMEM((2, feats + 8, e), F32),
                        pltpu.VMEM((2, feats + 8, e), F32), *stage(HT), *stage(RT),
                        pltpu.SemaphoreType.DMA((2, 6, 3, 4)), pltpu.SemaphoreType.DMA((2, 6, 3, 4)),
                        pltpu.SemaphoreType.DMA((2, 3)), pltpu.SemaphoreType.DMA((2,))],
        compiler_params=pltpu.CompilerParams(vmem_limit_bytes=56 * 2**20, collective_id=1, has_side_effects=True),
        name="second_bucket_and_sums",
    )(du, dr0, left1, ls1, right1, rs1, h1, r, q1, dqh1, heads, relations, tails, negatives)
    rel_new = apply(rel, relation_state, grel, 640, "relation_update")
    hub_new = apply(hub, hub_state, ghub, 512, "hub_update")
    return (left2.reshape(left_emb.shape), right2.reshape(right_emb.shape), rel_new.reshape(relation_emb.shape),
            hub_new.reshape(hub_emb.shape))


def solution(mesh):
    cut = P(None, None, ("blk", "sub"))
    row = P(("blk", "sub"))
    idx = P(None, ("blk", "sub"))
    return jax.shard_map(shards, mesh=mesh, in_specs=(cut, row, cut, row, P(), P(), P(), P(), idx, idx, idx, idx, idx),
                         out_specs=(cut, cut, P(), P()), check_vma=False)
```

```python
import functools
import jax
import jax.numpy as jnp
from jax import lax
from jax.experimental import pallas as pl
from jax.experimental.pallas import tpu as pltpu
from jax.sharding import PartitionSpec as P

RATE = 0.25
F32, BF16 = jnp.float32, jnp.bfloat16
NN = (((1,), (0,)), ((), ()))
NT = (((1,), (1,)), ((), ()))


def mm(a, b, dims=NN):
    return lax.dot_general(a, b, dims, preferred_element_type=F32)


def halves(x):
    hi = x.astype(BF16)
    return hi, (x - hi.astype(F32)).astype(BF16)


def stacked(x):
    hi, lo = halves(x)
    return jnp.concatenate([hi, lo], axis=0)


def mm3(a2, b_hi, b_lo, dims=NN):
    n = a2.shape[0] // 2
    both = mm(a2, b_hi, dims)
    return both[:n] + both[n:] + mm(a2[:n], b_lo, dims)


def fold(x):
    n = x.shape[0] // 2
    return x[:n] + x[n:]


def rows_hot(idx, base, count):
    at = lax.broadcasted_iota(jnp.int32, (count, idx.shape[1]), 0) + base
    return (at == idx).astype(F32).astype(BF16)


def column(idx):
    parts = []
    for k in range(0, idx.shape[1], 128):
        parts.append(jnp.broadcast_to(idx[:, k : k + 128], (128, 128)).T)
    return jnp.concatenate(parts, axis=0)


def lanes_hot(col, base, count):
    at = lax.broadcasted_iota(jnp.int32, (col.shape[0], 128), 1)
    return jnp.concatenate([col == at + (base + k) for k in range(0, count, 128)], axis=1)


def adagrad(table, state, grad):
    new_state = state + jnp.sum(grad * grad, axis=0, keepdims=True) * (1.0 / grad.shape[0])
    return table - grad * (RATE / jnp.sqrt(new_state)), new_state


def sigmoid(x):
    return 1.0 / (1.0 + jnp.exp(-x))


def cmul(a, b):
    n = a.shape[0] // 2
    a0, a1, b0, b1 = a[:n], a[n:], b[:n], b[n:]
    return jnp.concatenate([a0 * b0 - a1 * b1, a0 * b1 + a1 * b0], axis=0)


def cmul_conj(a, b):
    n = a.shape[0] // 2
    a0, a1, b0, b1 = a[:n], a[n:], b[:n], b[n:]
    return jnp.concatenate([a0 * b0 + a1 * b1, a1 * b0 - a0 * b1], axis=0)


def gather_loop(table_ref, idx, out_ref, block):
    count = table_ref.shape[1]
    out_ref[...] = jnp.zeros_like(out_ref)

    @pl.loop(0, count // block)
    def _(k):
        base = pl.multiple_of(k * block, block)
        out_ref[...] += mm(stacked(table_ref[:, pl.ds(base, block)]), rows_hot(idx, base, block))


def gather(table, idx):
    return mm(stacked(table), rows_hot(idx, 0, table.shape[1]))


def queries_side(q):
    qt = q.T
    return stacked(qt)


def coefs(score, w, tail_idx, neg_idx, rows):
    times = jnp.sum(rows_hot_f(neg_idx, rows), axis=1, keepdims=True)
    times = jnp.broadcast_to(times, (rows, 128)).T[0:1, :] * w
    tail = lanes_hot(column(tail_idx), 0, rows)
    s = sigmoid(score)
    return s * times + jnp.where(tail, s - 1.0, 0.0)


def rows_hot_f(idx, count):
    at = lax.broadcasted_iota(jnp.int32, (count, idx.shape[1]), 0)
    return (at == idx).astype(F32)


VMEM_MIB = 54
HUB_PARTS, REL_PARTS = (9, 8), (6,)
MESH = pl.DeviceIdType.MESH


class Sent:
    def __init__(self, src, dst, send_sem, recv_sem, dev, log):
        self.c = pltpu.make_async_remote_copy(src_ref=src, dst_ref=dst, send_sem=send_sem, recv_sem=recv_sem,
                                              device_id=dev, device_id_type=MESH)
        self.c.start()
        self.arrived = False
        log.append(self)

    def wait_recv(self):
        if not self.arrived:
            self.c.wait_recv()
            self.arrived = True

    def close(self):
        self.wait_recv()
        self.c.wait_send()


class Place:
    def __init__(self):
        b, s = lax.axis_index("blk"), lax.axis_index("sub")
        self.blk, self.sub = b, s
        self.core = lax.rem(b, 2)
        self.pos = [b // 4, lax.rem(b // 2, 2) * 2 + lax.rem(s, 2), s // 2]

    def at(self, pos, core):
        return ((pos[0] * 2 + pos[1] // 2) * 2 + core, pos[2] * 2 + lax.rem(pos[1], 2))

    def shift(self, axis, d):
        pos = list(self.pos)
        pos[axis] = lax.rem(pos[axis] + d, 4)
        return self.at(pos, self.core)

    def partition(self, d):
        return (lax.rem(self.blk + d, 16), self.sub)

    def sibling(self):
        return self.at(self.pos, 1 - self.core)


class Reduce:
    def __init__(self, place, n, off, g, full, rba, rbb, s1, rb2, s2, rb3, send_sems, recv_sems):
        self.p, self.n, self.off = place, n, off
        self.g, self.rba, self.rbb, self.s1, self.rb2, self.s2, self.rb3, self.full = g, rba, rbb, s1, rb2, s2, rb3, full
        self.send_sems, self.recv_sems = send_sems, recv_sems

    def put(self, step, part, src, dst, dev):
        pltpu.make_async_remote_copy(src_ref=src, dst_ref=dst, send_sem=self.send_sems.at[int(step == 8), part],
                                     recv_sem=self.recv_sems.at[step, part], device_id=dev,
                                     device_id_type=MESH).start()

    def got(self, step, part, tiles):
        ref = self.full.at[0, pl.ds(0, tiles)]
        pltpu.make_async_copy(ref, ref, self.recv_sems.at[step, part]).wait()

    def close(self):
        for part in range(3):
            for k, tiles in enumerate((33 * self.n, 16 * self.n)):
                ref = self.full.at[0, pl.ds(0, tiles)]
                pltpu.make_async_copy(ref, ref, self.send_sems.at[k, part]).wait()

    def axis(self, part, level):
        return (part + level) % 3

    def here(self, part, level):
        return self.p.pos[self.axis(part, level)]

    def half(self, part, c, k, level=0):
        return pl.ds(self.off + part * 16 * self.n + c * (4 * self.n) + k * (2 * self.n), 2 * self.n)

    def rs1(self, part):
        n, c, a = self.n, self.here(part, 0), self.axis(part, 0)
        for k, d in enumerate((1, 3)):
            self.put(0, part, self.g.at[self.half(part, lax.rem(c + 2, 4), k)], self.rba.at[part, k], self.p.shift(a, d))
        for k, d in enumerate((1, 3)):
            self.put(1, part, self.g.at[self.half(part, lax.rem(c + d, 4), 1 - k)],
                     self.rbb.at[part, k, pl.ds((1 - k) * 2 * n, 2 * n)], self.p.shift(a, d))

    def rs1_mid(self, part):
        n, c, a = self.n, self.here(part, 0), self.axis(part, 0)
        self.got(0, part, 4 * n)
        for k, d in enumerate((1, 3)):
            here = self.half(part, lax.rem(c + d, 4), k)
            self.g[here] = self.g[here] + self.rba[part, k]
            self.put(1, part, self.g.at[here], self.rbb.at[part, k, pl.ds(k * 2 * n, 2 * n)], self.p.shift(a, d))

    def rs1_done(self, part):
        n, c = self.n, self.here(part, 0)
        self.got(1, part, 8 * n)
        off = self.off + part * 16 * n + c * (4 * n)
        self.s1[part] = self.g[pl.ds(off, 4 * n)] + (self.rbb[part, 0] + self.rbb[part, 1])

    def rs2(self, part):
        n, c, a = self.n, self.here(part, 1), self.axis(part, 1)
        for d in (2, 1, 3):
            self.put(2, part, self.s1.at[part, pl.ds(lax.rem(c + d, 4) * n, n)], self.rb2.at[part, d - 1],
                     self.p.shift(a, d))

    def rs2_done(self, part):
        n, c = self.n, self.here(part, 1)
        self.got(2, part, 3 * n)
        self.s2[part] = (self.s1[part, pl.ds(c * n, n)] + self.rb2[part, 0]) + (self.rb2[part, 1] + self.rb2[part, 2])

    def ar3(self, part):
        c, a = self.here(part, 2), self.axis(part, 2)
        for d in (2, 1, 3):
            self.put(3, part, self.s2.at[part], self.rb3.at[part, c], self.p.shift(a, d))
        self.rb3[part, c] = self.s2[part]

    def mine(self, part):
        n = self.n
        return self.off + part * 16 * n + self.here(part, 0) * (4 * n) + self.here(part, 1) * n

    def ar3_done(self, part):
        self.got(3, part, 3 * self.n)
        self.full[self.p.core, pl.ds(self.mine(part), self.n)] = (
            (self.rb3[part, 0] + self.rb3[part, 1]) + (self.rb3[part, 2] + self.rb3[part, 3]))

    def ag2(self, part):
        a = self.axis(part, 1)
        ref = self.full.at[self.p.core, pl.ds(self.mine(part), self.n)]
        for d in (2, 1, 3):
            self.put(4, part, ref, ref, self.p.shift(a, d))

    def ag2_done(self, part):
        self.got(4, part, 3 * self.n)

    def chunk(self, part, c):
        return self.full.at[self.p.core, pl.ds(self.off + part * 16 * self.n + c * (4 * self.n), 4 * self.n)]

    def far(self, part, c, k):
        return self.full.at[self.p.core, self.half(part, c, k)]

    def ag1(self, part):
        c, a = self.here(part, 0), self.axis(part, 0)
        for j in range(2):
            for k, d in enumerate((1, 3)):
                ref = self.far(part, c, (k + j) % 2)
                self.put(5 + j, part, ref, ref, self.p.shift(a, d))
        ref = self.chunk(part, c)
        self.put(8, part, ref, ref, self.p.sibling())

    def ag1_mid(self, part):
        c, a = self.here(part, 0), self.axis(part, 0)
        self.got(5, part, 4 * self.n)
        for k, d in enumerate((1, 3)):
            ref = self.far(part, lax.rem(c + 4 - d, 4), k)
            self.put(7, part, ref, ref, self.p.shift(a, d))

    def ag1_near(self, part):
        c = self.here(part, 0)
        self.got(6, part, 4 * self.n)
        for k, d in enumerate((1, 3)):
            ref = self.chunk(part, lax.rem(c + 4 - d, 4))
            self.put(8, part, ref, ref, self.p.sibling())

    def ag1_done(self, part):
        c = self.here(part, 0)
        self.got(7, part, 4 * self.n)
        ref = self.chunk(part, lax.rem(c + 2, 4))
        self.put(8, part, ref, ref, self.p.sibling())

    def both(self, part):
        self.got(8, part, 16 * self.n)

    def each(self, *steps):
        for part in range(3):
            for step in steps:
                step(part)


def tiles_of(x):
    return [x[:, k : k + 128].reshape(x.shape[0] // 8, 8, 128) for k in range(0, x.shape[1], 128)]


def scatter_into(g_ref, at, grad2, col, base, width, add):
    hot = lanes_hot(col, base, width).astype(F32).astype(BF16)
    for j, t in enumerate(tiles_of(fold(mm(grad2, hot)))):
        n = t.shape[0]
        here = pl.ds(at + j * n, n)
        g_ref[here] = g_ref[here] + t if add else t


def buckets(w, left_ref, lstate_ref, right_ref, rstate_ref, rel_ref, relstate_ref, hub_ref, hstate_ref, heads_hbm, rels_hbm, tails_hbm,
            negs_hbm, hubs_hbm, left_out, right_out, hub_out, rel_out,
            left, lstate, right, rstate, rel, relstate, hub_t, hstate, heads, rels, tails, negs, hubs,
            r_buf, dut, dus, dro, drs, mout, min_, hg, hfull, rg, rfull, xsem, isem, osem, *batches):
    place = Place()
    log, loads = [], {}
    feats, rows = left.shape
    e = heads.shape[1]
    m = hubs.shape[1]
    for k, (name, src, dst) in enumerate((
            ("heads", heads_hbm, heads), ("rels", rels_hbm, rels), ("left", left_ref, left), ("rel", rel_ref, rel),
            ("right", right_ref, right), ("tails", tails_hbm, tails), ("negs", negs_hbm, negs),
            ("rstate", rstate_ref, rstate), ("lstate", lstate_ref, lstate), ("hubs", hubs_hbm, hubs),
            ("hub", hub_ref, hub_t), ("relstate", relstate_ref, relstate), ("hstate", hstate_ref, hstate))):
        loads[name] = pltpu.make_async_copy(src, dst, isem.at[k])
        if not name.startswith("hub"):
            loads[name].start()
    red = []
    for g, full, sizes in ((hg, hfull, HUB_PARTS), (rg, rfull, REL_PARTS)):
        off = 0
        for n in sizes:
            red.append(Reduce(place, n, off, g, full, *batches[8 * len(red) : 8 * len(red) + 8]))
            off += 48 * n
    ha, hb, rc = red
    barrier = pltpu.get_barrier_semaphore()
    for a in range(3):
        for d in (1, 2, 3):
            pl.semaphore_signal(barrier, inc=1, device_id=place.shift(a, d), device_id_type=MESH)
    for dev in (place.sibling(), place.partition(1), place.partition(15)):
        pl.semaphore_signal(barrier, inc=1, device_id=dev, device_id_type=MESH)

    def send(k, src, dst, dev):
        return Sent(src, dst, xsem.at[0, k], xsem.at[1, k], dev, log)

    for name in ("heads", "rels", "left", "rel"):
        loads[name].wait()
    loads["hub"].start()
    loads["hubs"].start()
    idx_r = jnp.concatenate([rels[0:1, :], rels[1:2, :]], axis=1)
    r_buf[...] = fold(mm(stacked(rel[...]), rows_hot(idx_r, 0, rel.shape[1])))
    h0 = fold(gather(left[...], heads[0:1, :]))
    q0 = cmul(h0, r_buf[:, :e])
    for name in ("right", "tails", "negs", "rstate"):
        loads[name].wait()
    q0t = stacked(q0.T)
    q02 = stacked(q0)
    r2 = stacked(right[...])
    coef = coefs(mm3(q0t, r2[:feats], r2[feats:]), w, tails[0:1, :], negs[0:1, :], rows)
    ch, cl = halves(coef)
    mout[:feats, :], state1 = adagrad(right[...], rstate[...], mm3(q02, ch, cl))
    mout[feats:, :] = jnp.broadcast_to(state1, (8, rows))
    pl.semaphore_wait(barrier, 12)
    x_m = send(3, mout, min_, place.partition(1))

    loads["hubs"].wait()
    loads["hub"].wait()
    idx_u = jnp.concatenate([hubs[0:1, :], hubs[1:2, :]], axis=1)
    u = mm(stacked(hub_t[...]), rows_hot(idx_u, 0, hub_t.shape[1])).astype(BF16)
    u0, u1 = u[:, :m], u[:, m:]
    ch2, cl2 = halves(sigmoid(mm3(q0t, u0[:feats], u0[feats:])) * w)
    dq = mm3(r2, ch, cl, NT) + mm3(u0, ch2, cl2, NT)
    dh = cmul_conj(dq, r_buf[:, :e])
    gl = fold(mm(stacked(dh), lanes_hot(column(heads[0:1, :]), 0, rows).astype(F32).astype(BF16)))
    loads["lstate"].wait()
    left[...], lstate[...] = adagrad(left[...], lstate[...], gl)
    dro[0, :feats, :] = cmul_conj(dq, h0)
    dro[0, feats:, :] = jnp.broadcast_to(rels[0:1, :].astype(F32), (8, e))
    x_r0 = send(1, dro.at[0], drs.at[0], place.sibling())
    h1 = fold(gather(left[...], heads[1:2, :]))
    q1 = cmul(h1, r_buf[:, e:])
    q1t = stacked(q1.T)
    q12 = stacked(q1)
    ch3, cl3 = halves(sigmoid(mm3(q1t, u1[:feats], u1[feats:])) * w)
    dut[:feats, :m] = mm3(q02, ch2, cl2)
    dut[:feats, m:] = mm3(q12, ch3, cl3)
    dut[feats:, :] = jnp.broadcast_to(idx_u.astype(F32), (8, 2 * m))
    x_u = send(0, dut, dus, place.sibling())

    half_lanes = hub_t.shape[1] // 2
    first_lane = place.core * half_lanes
    own2 = stacked(dut[:feats, :])
    own_col = column(idx_u)
    for k in range(4):
        scatter_into(hg, k * 200, own2, own_col, first_lane + k * 512, 512, False)
    hg[800:, :, :] = jnp.zeros((hg.shape[0] - 800, 8, 128), F32)
    x_u.wait_recv()
    sib2 = stacked(dus[:feats, :])
    sib_col = column(dus[feats : feats + 1, :].astype(jnp.int32))
    for k in range(4):
        scatter_into(hg, k * 200, sib2, sib_col, first_lane + k * 512, 512, True)
        if k == 2:
            ha.each(ha.rs1)
    hb.each(hb.rs1)
    dq1h = mm3(u1, ch3, cl3, NT)
    first_rel = place.core * (rel.shape[1] // 2)

    def rel_scatter(x, add):
        scatter_into(rg, 0, stacked(x[:feats, :]), column(x[feats : feats + 1, :].astype(jnp.int32)), first_rel, 640,
                     add)

    x_m.wait_recv()
    r2 = stacked(min_[:feats, :])
    coef = coefs(mm3(q1t, r2[:feats], r2[feats:]), w, tails[1:2, :], negs[1:2, :], rows)
    ha.each(ha.rs1_mid)
    ch, cl = halves(coef)
    dq = mm3(r2, ch, cl, NT) + dq1h
    dro[1, :feats, :] = cmul_conj(dq, h1)
    dro[1, feats:, :] = jnp.broadcast_to(rels[1:2, :].astype(F32), (8, e))
    x_r1 = send(2, dro.at[1], drs.at[1], place.sibling())
    hb.each(hb.rs1_mid)
    rel_scatter(dro[0], False)
    x_r0.wait_recv()
    rel_scatter(drs[0], True)
    rg[250:, :, :] = jnp.zeros((rg.shape[0] - 250, 8, 128), F32)
    rel_scatter(dro[1], True)
    x_r1.wait_recv()
    rel_scatter(drs[1], True)
    rc.each(rc.rs1)
    ha.each(ha.rs1_done, ha.rs2)
    g = mm3(q12, ch, cl)
    right_out[...], _ = adagrad(min_[:feats, :], min_[feats : feats + 1, :], g)
    rc.each(rc.rs1_mid)
    ha.each(ha.rs2_done, ha.ar3)
    hb.each(hb.rs1_done, hb.rs2)
    dh = cmul_conj(dq, r_buf[:, e:])
    gl = fold(mm(stacked(dh), lanes_hot(column(heads[1:2, :]), 0, rows).astype(F32).astype(BF16)))
    left_out[...], _ = adagrad(left[...], lstate[...], gl)
    ha.each(ha.ar3_done, ha.ag2)
    rc.each(rc.rs1_done, rc.rs2)
    hb.each(hb.rs2_done, hb.ar3)
    ha.each(ha.ag2_done, ha.ag1)
    rc.each(rc.rs2_done, rc.ar3)
    ha.each(ha.ag1_mid)
    hb.each(hb.ar3_done, hb.ag2)
    rc.each(rc.ar3_done, rc.ag2)
    hb.each(hb.ag2_done, hb.ag1)
    ha.each(ha.ag1_near)
    rc.each(rc.ag2_done, rc.ag1)
    hb.each(hb.ag1_mid)
    ha.each(ha.ag1_done)
    rc.each(rc.ag1_mid)
    hb.each(hb.ag1_near)
    loads["hstate"].wait()
    loads["relstate"].wait()
    outs = []

    def final(table, state, full, out, at, number, lanes):
        n = feats // 8
        count = lanes // 2 // 128
        for h in range(2):
            for j in range(at, at + number):
                here = slice((h * count + j) * 128, (h * count + j + 1) * 128)
                gj = full[h, j * n : (j + 1) * n].reshape(feats, 128)
                new = state[h * count + j : h * count + j + 1, :] + jnp.sum(gj * gj, axis=0, keepdims=True) * (1.0 / feats)
                table[:, here] = table[:, here] - gj * (RATE / jnp.sqrt(new))
            here = pl.ds((h * count + at) * 128, number * 128)
            outs.append(pltpu.make_async_copy(table.at[:, here], out.at[:, here], osem.at[len(outs)]))
            outs[-1].start()

    ha.each(ha.both)
    final(hub_t, hstate, hfull, hub_out, 0, 8, hub_t.shape[1])
    hb.each(hb.ag1_done)
    rc.each(rc.ag1_near)
    rc.each(rc.ag1_done)
    hb.each(hb.both)
    final(hub_t, hstate, hfull, hub_out, 8, 8, hub_t.shape[1])
    rc.each(rc.both)
    final(rel, relstate, rfull, rel_out, 0, 5, rel.shape[1])
    for c in log + red:
        c.close()
    for c in outs:
        c.wait()


def hand_on(*refs):
    n = (len(refs) - 1) // 3
    steps = []
    for src, dst, mid in zip(refs[:n], refs[n : 2 * n], refs[2 * n : 3 * n]):
        cut = src.shape[0] // 5
        for k in range(5):
            here = pl.ds(k * cut, cut)
            sem = refs[-1].at[len(steps)]
            steps.append((pltpu.make_async_copy(src.at[here], mid.at[here], sem),
                          pltpu.make_async_copy(mid.at[here], dst.at[here], sem)))
            steps[-1][0].start()
    for load, store in steps:
        load.wait()
        store.start()
    for load, store in steps:
        store.wait()


def shards(left_emb, left_state, right_emb, right_state, relation_emb, relation_state, hub_emb, hub_state, heads,
           relations, tails, negatives, hub_ids):
    two, half, rows = left_emb.shape
    feats = two * half
    e = heads.shape[1]
    m = hub_ids.shape[1]
    w = 1.0 / (negatives.shape[1] + hub_ids.shape[1])
    left = left_emb.reshape(feats, rows)
    right = right_emb.reshape(feats, rows)
    rel = relation_emb.reshape(feats, -1)
    hub = hub_emb.reshape(feats, -1)
    sd = lambda *s: jax.ShapeDtypeStruct(s, F32)
    vm = pl.BlockSpec(memory_space=pltpu.VMEM)
    hbm = pl.BlockSpec(memory_space=pl.ANY)
    tile = lambda *s: pltpu.VMEM((*s, 8, 128), F32)
    fl = lambda *s: pltpu.VMEM(s, F32)
    it = lambda *s: pltpu.VMEM(s, jnp.int32)
    dma = pltpu.SemaphoreType.DMA
    batch = lambda n: [tile(3, 2, 2 * n), tile(3, 2, 4 * n), tile(3, 4 * n), tile(3, 3, n), tile(3, n), tile(3, 4, n),
                       dma((2, 3)), dma((9, 3))]
    ht, rt = 48 * sum(HUB_PARTS), 48 * sum(REL_PARTS)
    outs = [sd(feats, rows), sd(feats, rows), sd(*hub.shape), sd(*rel.shape)]
    left2, right2, hub_new, rel_new = pl.pallas_call(
        functools.partial(buckets, w), out_shape=outs, in_specs=[hbm] * 13, out_specs=[vm, vm, hbm, hbm],
        scratch_shapes=[
            fl(feats, rows), fl(1, rows), fl(feats, rows), fl(1, rows), fl(feats, rel.shape[1]),
            fl(rel.shape[1] // 128, 128), fl(feats, hub.shape[1]), fl(hub.shape[1] // 128, 128),
            it(2, e), it(2, e), it(2, e), it(2, negatives.shape[1]), it(2, m),
            fl(feats, 2 * e), fl(feats + 8, 2 * m), fl(feats + 8, 2 * m), fl(2, feats + 8, e), fl(2, feats + 8, e),
            fl(feats + 8, rows), fl(feats + 8, rows), tile(ht), tile(2, ht), tile(rt), tile(2, rt),
            dma((2, 4)), dma((13,)), dma((6,)), *(x for n in HUB_PARTS + REL_PARTS for x in batch(n))],
        compiler_params=pltpu.CompilerParams(vmem_limit_bytes=VMEM_MIB * 2**20, collective_id=1, has_side_effects=True),
        name="buckets",
    )(left, left_state[None], right, right_state[None], rel, relation_state.reshape(-1, 128), hub,
      hub_state.reshape(-1, 128), heads, relations, tails, negatives, hub_ids)
    outs = [left2, right2, rel_new, hub_new]
    left2, right2, rel_new, hub_new = pl.pallas_call(
        hand_on, out_shape=[sd(*x.shape) for x in outs], in_specs=[hbm] * 4, out_specs=[hbm] * 4,
        scratch_shapes=[*(fl(*x.shape) for x in outs), dma((len(outs) * 5,))], name="hand_on",
        compiler_params=pltpu.CompilerParams(vmem_limit_bytes=60 * 2**20),
    )(*outs)
    return (left2.reshape(left_emb.shape), right2.reshape(right_emb.shape), rel_new.reshape(relation_emb.shape),
            hub_new.reshape(hub_emb.shape))


def solution(mesh):
    cut = P(None, None, ("blk", "sub"))
    row = P(("blk", "sub"))
    idx = P(None, ("blk", "sub"))
    return jax.shard_map(shards, mesh=mesh, in_specs=(cut, row, cut, row, P(), P(), P(), P(), idx, idx, idx, idx, idx),
                         out_specs=(cut, cut, P(), P()), check_vma=False)
```

```python
import functools
import jax
import jax.numpy as jnp
from jax import lax
from jax.experimental import pallas as pl
from jax.experimental.pallas import tpu as pltpu
from jax.sharding import PartitionSpec as P

RATE = 0.25
F32, BF16 = jnp.float32, jnp.bfloat16
NN = (((1,), (0,)), ((), ()))
NT = (((1,), (1,)), ((), ()))


def mm(a, b, dims=NN):
    return lax.dot_general(a, b, dims, preferred_element_type=F32)


def halves(x):
    hi = x.astype(BF16)
    return hi, (x - hi.astype(F32)).astype(BF16)


def stacked(x):
    hi, lo = halves(x)
    return jnp.concatenate([hi, lo], axis=0)


def mm3(a2, b_hi, b_lo, dims=NN):
    n = a2.shape[0] // 2
    both = mm(a2, b_hi, dims)
    return both[:n] + both[n:] + mm(a2[:n], b_lo, dims)


def fold(x):
    n = x.shape[0] // 2
    return x[:n] + x[n:]


def rows_hot(idx, base, count):
    at = lax.broadcasted_iota(jnp.int32, (count, idx.shape[1]), 0) + base
    return (at == idx).astype(F32).astype(BF16)


def column(idx):
    parts = []
    for k in range(0, idx.shape[1], 128):
        parts.append(jnp.broadcast_to(idx[:, k : k + 128], (128, 128)).T)
    return jnp.concatenate(parts, axis=0)


def lanes_hot(col, base, count):
    at = lax.broadcasted_iota(jnp.int32, (col.shape[0], 128), 1)
    return jnp.concatenate([col == at + (base + k) for k in range(0, count, 128)], axis=1)


def adagrad(table, state, grad):
    new_state = state + jnp.sum(grad * grad, axis=0, keepdims=True) * (1.0 / grad.shape[0])
    return table - grad * (RATE / jnp.sqrt(new_state)), new_state


def sigmoid(x):
    return 1.0 / (1.0 + jnp.exp(-x))


def cmul(a, b):
    n = a.shape[0] // 2
    a0, a1, b0, b1 = a[:n], a[n:], b[:n], b[n:]
    return jnp.concatenate([a0 * b0 - a1 * b1, a0 * b1 + a1 * b0], axis=0)


def cmul_conj(a, b):
    n = a.shape[0] // 2
    a0, a1, b0, b1 = a[:n], a[n:], b[:n], b[n:]
    return jnp.concatenate([a0 * b0 + a1 * b1, a1 * b0 - a0 * b1], axis=0)


def gather_loop(table_ref, idx, out_ref, block):
    count = table_ref.shape[1]
    out_ref[...] = jnp.zeros_like(out_ref)

    @pl.loop(0, count // block)
    def _(k):
        base = pl.multiple_of(k * block, block)
        out_ref[...] += mm(stacked(table_ref[:, pl.ds(base, block)]), rows_hot(idx, base, block))


def gather(table, idx):
    return mm(stacked(table), rows_hot(idx, 0, table.shape[1]))


def queries_side(q):
    qt = q.T
    return stacked(qt)


def coefs(score, w, tail_idx, neg_idx, rows):
    times = jnp.sum(rows_hot_f(neg_idx, rows), axis=1, keepdims=True)
    times = jnp.broadcast_to(times, (rows, 128)).T[0:1, :] * w
    tail = lanes_hot(column(tail_idx), 0, rows)
    s = sigmoid(score)
    return s * times + jnp.where(tail, s - 1.0, 0.0)


def rows_hot_f(idx, count):
    at = lax.broadcasted_iota(jnp.int32, (count, idx.shape[1]), 0)
    return (at == idx).astype(F32)


VMEM_MIB = 54
PARTS = (8, 8, 6)
MESH = pl.DeviceIdType.MESH


class Sent:
    def __init__(self, src, dst, send_sem, recv_sem, dev, log):
        self.c = pltpu.make_async_remote_copy(src_ref=src, dst_ref=dst, send_sem=send_sem, recv_sem=recv_sem,
                                              device_id=dev, device_id_type=MESH)
        self.c.start()
        self.arrived = False
        log.append(self)

    def wait_recv(self):
        if not self.arrived:
            self.c.wait_recv()
            self.arrived = True

    def close(self):
        self.wait_recv()
        self.c.wait_send()


class Place:
    def __init__(self):
        b, s = lax.axis_index("blk"), lax.axis_index("sub")
        self.blk, self.sub = b, s
        self.core = lax.rem(b, 2)
        self.pos = [b // 4, lax.rem(b // 2, 2) * 2 + lax.rem(s, 2), s // 2]

    def at(self, pos, core):
        return ((pos[0] * 2 + pos[1] // 2) * 2 + core, pos[2] * 2 + lax.rem(pos[1], 2))

    def shift(self, axis, d):
        pos = list(self.pos)
        pos[axis] = lax.rem(pos[axis] + d, 4)
        return self.at(pos, self.core)

    def partition(self, d):
        return (lax.rem(self.blk + d, 16), self.sub)

    def sibling(self):
        return self.at(self.pos, 1 - self.core)


class Reduce:
    def __init__(self, place, n, off, g, full, rba, rbb, s1, rb2, s2, rb3, send_sems, recv_sems):
        self.p, self.n, self.off = place, n, off
        self.g, self.rba, self.rbb, self.s1, self.rb2, self.s2, self.rb3, self.full = g, rba, rbb, s1, rb2, s2, rb3, full
        self.send_sems, self.recv_sems = send_sems, recv_sems

    def put(self, step, part, src, dst, dev):
        pltpu.make_async_remote_copy(src_ref=src, dst_ref=dst, send_sem=self.send_sems.at[int(step == 8), part],
                                     recv_sem=self.recv_sems.at[step, part], device_id=dev,
                                     device_id_type=MESH).start()

    def got(self, step, part, tiles):
        ref = self.full.at[0, pl.ds(0, tiles)]
        pltpu.make_async_copy(ref, ref, self.recv_sems.at[step, part]).wait()

    def close(self):
        for part in range(3):
            for k, tiles in enumerate((33 * self.n, 16 * self.n)):
                ref = self.full.at[0, pl.ds(0, tiles)]
                pltpu.make_async_copy(ref, ref, self.send_sems.at[k, part]).wait()

    def axis(self, part, level):
        return (part + level) % 3

    def here(self, part, level):
        return self.p.pos[self.axis(part, level)]

    def half(self, part, c, k, level=0):
        return pl.ds(self.off + part * 16 * self.n + c * (4 * self.n) + k * (2 * self.n), 2 * self.n)

    def rs1(self, part):
        n, c, a = self.n, self.here(part, 0), self.axis(part, 0)
        for k, d in enumerate((1, 3)):
            self.put(0, part, self.g.at[self.half(part, lax.rem(c + 2, 4), k)], self.rba.at[part, k], self.p.shift(a, d))
        for k, d in enumerate((1, 3)):
            self.put(1, part, self.g.at[self.half(part, lax.rem(c + d, 4), 1 - k)],
                     self.rbb.at[part, k, pl.ds((1 - k) * 2 * n, 2 * n)], self.p.shift(a, d))

    def rs1_mid(self, part):
        n, c, a = self.n, self.here(part, 0), self.axis(part, 0)
        self.got(0, part, 4 * n)
        for k, d in enumerate((1, 3)):
            here = self.half(part, lax.rem(c + d, 4), k)
            self.g[here] = self.g[here] + self.rba[part, k]
            self.put(1, part, self.g.at[here], self.rbb.at[part, k, pl.ds(k * 2 * n, 2 * n)], self.p.shift(a, d))

    def rs1_done(self, part):
        n, c = self.n, self.here(part, 0)
        self.got(1, part, 8 * n)
        off = self.off + part * 16 * n + c * (4 * n)
        self.s1[part] = self.g[pl.ds(off, 4 * n)] + (self.rbb[part, 0] + self.rbb[part, 1])

    def rs2(self, part):
        n, c, a = self.n, self.here(part, 1), self.axis(part, 1)
        for d in (2, 1, 3):
            self.put(2, part, self.s1.at[part, pl.ds(lax.rem(c + d, 4) * n, n)], self.rb2.at[part, d - 1],
                     self.p.shift(a, d))

    def rs2_done(self, part):
        n, c = self.n, self.here(part, 1)
        self.got(2, part, 3 * n)
        self.s2[part] = (self.s1[part, pl.ds(c * n, n)] + self.rb2[part, 0]) + (self.rb2[part, 1] + self.rb2[part, 2])

    def ar3(self, part):
        c, a = self.here(part, 2), self.axis(part, 2)
        for d in (2, 1, 3):
            self.put(3, part, self.s2.at[part], self.rb3.at[part, c], self.p.shift(a, d))
        self.rb3[part, c] = self.s2[part]

    def mine(self, part):
        n = self.n
        return self.off + part * 16 * n + self.here(part, 0) * (4 * n) + self.here(part, 1) * n

    def ar3_done(self, part):
        self.got(3, part, 3 * self.n)
        self.full[self.p.core, pl.ds(self.mine(part), self.n)] = (
            (self.rb3[part, 0] + self.rb3[part, 1]) + (self.rb3[part, 2] + self.rb3[part, 3]))

    def ag2(self, part):
        a = self.axis(part, 1)
        ref = self.full.at[self.p.core, pl.ds(self.mine(part), self.n)]
        for d in (2, 1, 3):
            self.put(4, part, ref, ref, self.p.shift(a, d))

    def ag2_done(self, part):
        self.got(4, part, 3 * self.n)

    def chunk(self, part, c):
        return self.full.at[self.p.core, pl.ds(self.off + part * 16 * self.n + c * (4 * self.n), 4 * self.n)]

    def far(self, part, c, k):
        return self.full.at[self.p.core, self.half(part, c, k)]

    def ag1(self, part):
        c, a = self.here(part, 0), self.axis(part, 0)
        for j in range(2):
            for k, d in enumerate((1, 3)):
                ref = self.far(part, c, (k + j) % 2)
                self.put(5 + j, part, ref, ref, self.p.shift(a, d))
        ref = self.chunk(part, c)
        self.put(8, part, ref, ref, self.p.sibling())

    def ag1_mid(self, part):
        c, a = self.here(part, 0), self.axis(part, 0)
        self.got(5, part, 4 * self.n)
        for k, d in enumerate((1, 3)):
            ref = self.far(part, lax.rem(c + 4 - d, 4), k)
            self.put(7, part, ref, ref, self.p.shift(a, d))

    def ag1_near(self, part):
        c = self.here(part, 0)
        self.got(6, part, 4 * self.n)
        for k, d in enumerate((1, 3)):
            ref = self.chunk(part, lax.rem(c + 4 - d, 4))
            self.put(8, part, ref, ref, self.p.sibling())

    def ag1_done(self, part):
        c = self.here(part, 0)
        self.got(7, part, 4 * self.n)
        ref = self.chunk(part, lax.rem(c + 2, 4))
        self.put(8, part, ref, ref, self.p.sibling())

    def both(self, part):
        self.got(8, part, 16 * self.n)

    def each(self, *steps):
        for part in range(3):
            for step in steps:
                step(part)


def tiles_of(x):
    return [x[:, k : k + 128].reshape(x.shape[0] // 8, 8, 128) for k in range(0, x.shape[1], 128)]


def scatter_into(g_ref, at, grad2, col, base, width, add):
    hot = lanes_hot(col, base, width).astype(F32).astype(BF16)
    for j, t in enumerate(tiles_of(fold(mm(grad2, hot)))):
        n = t.shape[0]
        here = pl.ds(at + j * n, n)
        g_ref[here] = g_ref[here] + t if add else t


def buckets(w, left_ref, lstate_ref, right_ref, rstate_ref, rel_ref, relstate_ref, hub_ref, hstate_ref, heads_hbm, rels_hbm, tails_hbm,
            negs_hbm, hubs_hbm, left_out, right_out, hub_t, rel,
            left, lstate, right, rstate, relstate, hstate, heads, rels, tails, negs, hubs,
            r_buf, dut, dus, dro, drs, mout, min_, g, full, xsem, isem, *batches):
    place = Place()
    log, loads = [], {}
    feats, rows = left.shape
    e = heads.shape[1]
    m = hubs.shape[1]
    for k, (name, src, dst) in enumerate((
            ("rels", rels_hbm, rels), ("heads", heads_hbm, heads), ("rel", rel_ref, rel), ("left", left_ref, left),
            ("right", right_ref, right), ("tails", tails_hbm, tails), ("negs", negs_hbm, negs),
            ("rstate", rstate_ref, rstate), ("lstate", lstate_ref, lstate), ("hubs", hubs_hbm, hubs),
            ("hub", hub_ref, hub_t), ("relstate", relstate_ref, relstate), ("hstate", hstate_ref, hstate))):
        loads[name] = pltpu.make_async_copy(src, dst, isem.at[k])
        if not name.startswith("hub"):
            loads[name].start()
    hub_tiles = feats // 8 * (hub_t.shape[1] // 256)
    rel_tiles = feats // 8 * (rel.shape[1] // 256)
    red, off = [], 0
    for n in PARTS:
        red.append(Reduce(place, n, off, g, full, *batches[8 * len(red) : 8 * len(red) + 8]))
        off += 48 * n
    ha, hb, rc = red
    barrier = pltpu.get_barrier_semaphore()
    for a in range(3):
        for d in (1, 2, 3):
            pl.semaphore_signal(barrier, inc=1, device_id=place.shift(a, d), device_id_type=MESH)
    for dev in (place.sibling(), place.partition(1), place.partition(15)):
        pl.semaphore_signal(barrier, inc=1, device_id=dev, device_id_type=MESH)

    def send(k, src, dst, dev):
        return Sent(src, dst, xsem.at[0, k], xsem.at[1, k], dev, log)

    for name in ("heads", "rels", "left", "rel"):
        loads[name].wait()
    loads["hub"].start()
    loads["hubs"].start()
    idx_r = jnp.concatenate([rels[0:1, :], rels[1:2, :]], axis=1)
    r_buf[...] = fold(mm(stacked(rel[...]), rows_hot(idx_r, 0, rel.shape[1])))
    h0 = fold(gather(left[...], heads[0:1, :]))
    q0 = cmul(h0, r_buf[:, :e])
    for name in ("right", "tails", "negs", "rstate"):
        loads[name].wait()
    q0t = stacked(q0.T)
    q02 = stacked(q0)
    r2 = stacked(right[...])
    coef = coefs(mm3(q0t, r2[:feats], r2[feats:]), w, tails[0:1, :], negs[0:1, :], rows)
    ch, cl = halves(coef)
    mout[:feats, :], state1 = adagrad(right[...], rstate[...], mm3(q02, ch, cl))
    mout[feats:, :] = jnp.broadcast_to(state1, (8, rows))
    pl.semaphore_wait(barrier, 12)
    x_m = send(3, mout, min_, place.partition(1))

    loads["hubs"].wait()
    loads["hub"].wait()
    idx_u = jnp.concatenate([hubs[0:1, :], hubs[1:2, :]], axis=1)
    u = mm(stacked(hub_t[...]), rows_hot(idx_u, 0, hub_t.shape[1])).astype(BF16)
    u0, u1 = u[:, :m], u[:, m:]
    ch2, cl2 = halves(sigmoid(mm3(q0t, u0[:feats], u0[feats:])) * w)
    dq = mm3(r2, ch, cl, NT) + mm3(u0, ch2, cl2, NT)
    dh = cmul_conj(dq, r_buf[:, :e])
    gl = fold(mm(stacked(dh), lanes_hot(column(heads[0:1, :]), 0, rows).astype(F32).astype(BF16)))
    loads["lstate"].wait()
    left[...], lstate[...] = adagrad(left[...], lstate[...], gl)
    dro[0, :feats, :] = cmul_conj(dq, h0)
    dro[0, feats:, :] = jnp.broadcast_to(rels[0:1, :].astype(F32), (8, e))
    x_r0 = send(1, dro.at[0], drs.at[0], place.sibling())
    h1 = fold(gather(left[...], heads[1:2, :]))
    q1 = cmul(h1, r_buf[:, e:])
    q1t = stacked(q1.T)
    q12 = stacked(q1)
    ch3, cl3 = halves(sigmoid(mm3(q1t, u1[:feats], u1[feats:])) * w)
    dut[:feats, :m] = mm3(q02, ch2, cl2)
    dut[:feats, m:] = mm3(q12, ch3, cl3)
    dut[feats:, :] = jnp.broadcast_to(idx_u.astype(F32), (8, 2 * m))
    x_u = send(0, dut, dus, place.sibling())

    half_lanes = hub_t.shape[1] // 2
    first_lane = place.core * half_lanes
    own2 = stacked(dut[:feats, :])
    own_col = column(idx_u)
    for k in range(4):
        scatter_into(g, k * 200, own2, own_col, first_lane + k * 512, 512, False)
    g[hub_tiles + rel_tiles :] = jnp.zeros((g.shape[0] - hub_tiles - rel_tiles, 8, 128), F32)
    x_u.wait_recv()
    sib2 = stacked(dus[:feats, :])
    sib_col = column(dus[feats : feats + 1, :].astype(jnp.int32))
    for k in range(4):
        scatter_into(g, k * 200, sib2, sib_col, first_lane + k * 512, 512, True)
        if k == 1:
            ha.each(ha.rs1)
    hb.each(hb.rs1)
    dq1h = mm3(u1, ch3, cl3, NT)
    first_rel = place.core * (rel.shape[1] // 2)

    def rel_scatter(x, add):
        scatter_into(g, hub_tiles, stacked(x[:feats, :]), column(x[feats : feats + 1, :].astype(jnp.int32)), first_rel, 640,
                     add)

    x_m.wait_recv()
    r2 = stacked(min_[:feats, :])
    coef = coefs(mm3(q1t, r2[:feats], r2[feats:]), w, tails[1:2, :], negs[1:2, :], rows)
    ha.each(ha.rs1_mid)
    ch, cl = halves(coef)
    dq = mm3(r2, ch, cl, NT) + dq1h
    dro[1, :feats, :] = cmul_conj(dq, h1)
    dro[1, feats:, :] = jnp.broadcast_to(rels[1:2, :].astype(F32), (8, e))
    x_r1 = send(2, dro.at[1], drs.at[1], place.sibling())
    hb.each(hb.rs1_mid)
    rel_scatter(dro[0], False)
    x_r0.wait_recv()
    rel_scatter(drs[0], True)
    rel_scatter(dro[1], True)
    x_r1.wait_recv()
    rel_scatter(drs[1], True)
    rc.each(rc.rs1)
    ha.each(ha.rs1_done, ha.rs2)
    right_out[...], _ = adagrad(min_[:feats, :], min_[feats : feats + 1, :], mm3(q12, ch, cl))
    hb.each(hb.rs1_done, hb.rs2)
    rc.each(rc.rs1_mid)
    ha.each(ha.rs2_done, ha.ar3)
    dh = cmul_conj(dq, r_buf[:, e:])
    gl = fold(mm(stacked(dh), lanes_hot(column(heads[1:2, :]), 0, rows).astype(F32).astype(BF16)))
    left_out[...], _ = adagrad(left[...], lstate[...], gl)
    hb.each(hb.rs2_done, hb.ar3)
    rc.each(rc.rs1_done, rc.rs2)
    ha.each(ha.ar3_done, ha.ag2)
    hb.each(hb.ar3_done, hb.ag2)
    rc.each(rc.rs2_done, rc.ar3)
    ha.each(ha.ag2_done, ha.ag1)
    hb.each(hb.ag2_done, hb.ag1)
    rc.each(rc.ar3_done, rc.ag2)
    ha.each(ha.ag1_mid)
    hb.each(hb.ag1_mid)
    rc.each(rc.ag2_done, rc.ag1)
    ha.each(ha.ag1_near)
    hb.each(hb.ag1_near)
    rc.each(rc.ag1_mid)
    ha.each(ha.ag1_done)
    loads["hstate"].wait()
    loads["relstate"].wait()

    def final(table, state, first_tile, at, number, lanes):
        n = feats // 8
        count = lanes // 2 // 128
        for h in range(2):
            for j in range(at, at + number):
                here = slice((h * count + j) * 128, (h * count + j + 1) * 128)
                gj = full[h, first_tile + j * n : first_tile + (j + 1) * n].reshape(feats, 128)
                new = state[h * count + j : h * count + j + 1, :] + jnp.sum(gj * gj, axis=0, keepdims=True) * (1.0 / feats)
                table[:, here] = table[:, here] - gj * (RATE / jnp.sqrt(new))

    ha.each(ha.both)
    final(hub_t, hstate, 0, 0, 7, hub_t.shape[1])
    hb.each(hb.ag1_done)
    rc.each(rc.ag1_near)
    rc.each(rc.ag1_done)
    hb.each(hb.both)
    final(hub_t, hstate, 0, 7, 8, hub_t.shape[1])
    rc.each(rc.both)
    final(hub_t, hstate, 0, 15, 1, hub_t.shape[1])
    final(rel, relstate, hub_tiles, 0, 5, rel.shape[1])
    for c in log + red:
        c.close()


def hand_on(*refs):
    n = (len(refs) - 1) // 2
    copies = []
    for src, dst in zip(refs[:n], refs[n : 2 * n]):
        cut = src.shape[0] // 5
        for k in range(5):
            here = pl.ds(k * cut, cut)
            copies.append(pltpu.make_async_copy(src.at[here], dst.at[here], refs[-1].at[len(copies)]))
            copies[-1].start()
    for c in copies:
        c.wait()


def shards(left_emb, left_state, right_emb, right_state, relation_emb, relation_state, hub_emb, hub_state, heads,
           relations, tails, negatives, hub_ids):
    two, half, rows = left_emb.shape
    feats = two * half
    e = heads.shape[1]
    m = hub_ids.shape[1]
    w = 1.0 / (negatives.shape[1] + hub_ids.shape[1])
    left = left_emb.reshape(feats, rows)
    right = right_emb.reshape(feats, rows)
    rel = relation_emb.reshape(feats, -1)
    hub = hub_emb.reshape(feats, -1)
    sd = lambda *s: jax.ShapeDtypeStruct(s, F32)
    vm = pl.BlockSpec(memory_space=pltpu.VMEM)
    hbm = pl.BlockSpec(memory_space=pl.ANY)
    tile = lambda *s: pltpu.VMEM((*s, 8, 128), F32)
    fl = lambda *s: pltpu.VMEM(s, F32)
    it = lambda *s: pltpu.VMEM(s, jnp.int32)
    dma = pltpu.SemaphoreType.DMA
    batch = lambda n: [tile(3, 2, 2 * n), tile(3, 2, 4 * n), tile(3, 4 * n), tile(3, 3, n), tile(3, n), tile(3, 4, n),
                       dma((2, 3)), dma((9, 3))]
    total = 48 * sum(PARTS)
    outs = [fl(feats, rows), fl(feats, rows), fl(*hub.shape), fl(*rel.shape)]
    left2, right2, hub_new, rel_new = pl.pallas_call(
        functools.partial(buckets, w), out_shape=outs, in_specs=[hbm] * 13, out_specs=[vm] * 4,
        scratch_shapes=[
            fl(feats, rows), fl(1, rows), fl(feats, rows), fl(1, rows),
            fl(rel.shape[1] // 128, 128), fl(hub.shape[1] // 128, 128),
            it(2, e), it(2, e), it(2, e), it(2, negatives.shape[1]), it(2, m),
            fl(feats, 2 * e), fl(feats + 8, 2 * m), fl(feats + 8, 2 * m), fl(2, feats + 8, e), fl(2, feats + 8, e),
            fl(feats + 8, rows), fl(feats + 8, rows), tile(total), tile(2, total),
            dma((2, 4)), dma((13,)), *(x for n in PARTS for x in batch(n))],
        compiler_params=pltpu.CompilerParams(vmem_limit_bytes=VMEM_MIB * 2**20, collective_id=1, has_side_effects=True),
        name="buckets",
    )(left, left_state[None], right, right_state[None], rel, relation_state.reshape(-1, 128), hub,
      hub_state.reshape(-1, 128), heads, relations, tails, negatives, hub_ids)
    outs = [left2, right2, rel_new, hub_new]
    left2, right2, rel_new, hub_new = pl.pallas_call(
        hand_on, out_shape=[sd(*x.shape) for x in outs], in_specs=[vm] * 4, out_specs=[hbm] * 4,
        scratch_shapes=[dma((len(outs) * 5,))], name="hand_on",
        compiler_params=pltpu.CompilerParams(vmem_limit_bytes=4 * 2**20),
    )(*(pltpu.with_memory_space_constraint(x, pltpu.VMEM) for x in outs))
    return (left2.reshape(left_emb.shape), right2.reshape(right_emb.shape), rel_new.reshape(relation_emb.shape),
            hub_new.reshape(hub_emb.shape))


def solution(mesh):
    cut = P(None, None, ("blk", "sub"))
    row = P(("blk", "sub"))
    idx = P(None, ("blk", "sub"))
    return jax.shard_map(shards, mesh=mesh, in_specs=(cut, row, cut, row, P(), P(), P(), P(), idx, idx, idx, idx, idx),
                         out_specs=(cut, cut, P(), P()), check_vma=False)
```

```python
import functools
import jax
import jax.numpy as jnp
from jax import lax
from jax.experimental import pallas as pl
from jax.experimental.pallas import tpu as pltpu
from jax.sharding import PartitionSpec as P

RATE = 0.25
F32, BF16 = jnp.float32, jnp.bfloat16
NN = (((1,), (0,)), ((), ()))
NT = (((1,), (1,)), ((), ()))


def mm(a, b, dims=NN):
    return lax.dot_general(a, b, dims, preferred_element_type=F32)


def halves(x):
    hi = x.astype(BF16)
    return hi, (x - hi.astype(F32)).astype(BF16)


def stacked(x):
    hi, lo = halves(x)
    return jnp.concatenate([hi, lo], axis=0)


def mm3(a2, b_hi, b_lo, dims=NN):
    n = a2.shape[0] // 2
    both = mm(a2, b_hi, dims)
    return both[:n] + both[n:] + mm(a2[:n], b_lo, dims)


def fold(x):
    n = x.shape[0] // 2
    return x[:n] + x[n:]


def rows_hot(idx, base, count):
    at = lax.broadcasted_iota(jnp.int32, (count, idx.shape[1]), 0) + base
    return (at == idx).astype(F32).astype(BF16)


def column(idx):
    parts = []
    for k in range(0, idx.shape[1], 128):
        parts.append(jnp.broadcast_to(idx[:, k : k + 128], (128, 128)).T)
    return jnp.concatenate(parts, axis=0)


def lanes_hot(col, base, count):
    at = lax.broadcasted_iota(jnp.int32, (col.shape[0], 128), 1)
    return jnp.concatenate([col == at + (base + k) for k in range(0, count, 128)], axis=1)


def adagrad(table, state, grad):
    new_state = state + jnp.sum(grad * grad, axis=0, keepdims=True) * (1.0 / grad.shape[0])
    return table - grad * (RATE / jnp.sqrt(new_state)), new_state


def sigmoid(x):
    return 1.0 / (1.0 + jnp.exp(-x))


def cmul(a, b):
    n = a.shape[0] // 2
    a0, a1, b0, b1 = a[:n], a[n:], b[:n], b[n:]
    return jnp.concatenate([a0 * b0 - a1 * b1, a0 * b1 + a1 * b0], axis=0)


def cmul_conj(a, b):
    n = a.shape[0] // 2
    a0, a1, b0, b1 = a[:n], a[n:], b[:n], b[n:]
    return jnp.concatenate([a0 * b0 + a1 * b1, a1 * b0 - a0 * b1], axis=0)


def gather_loop(table_ref, idx, out_ref, block):
    count = table_ref.shape[1]
    out_ref[...] = jnp.zeros_like(out_ref)

    @pl.loop(0, count // block)
    def _(k):
        base = pl.multiple_of(k * block, block)
        out_ref[...] += mm(stacked(table_ref[:, pl.ds(base, block)]), rows_hot(idx, base, block))


def gather(table, idx):
    return mm(stacked(table), rows_hot(idx, 0, table.shape[1]))


def queries_side(q):
    qt = q.T
    return stacked(qt)


def coefs(score, w, tail_idx, neg_idx, rows):
    times = jnp.sum(rows_hot_f(neg_idx, rows), axis=1, keepdims=True)
    times = jnp.broadcast_to(times, (rows, 128)).T[0:1, :] * w
    tail = lanes_hot(column(tail_idx), 0, rows)
    s = sigmoid(score)
    return s * times + jnp.where(tail, s - 1.0, 0.0)


def rows_hot_f(idx, count):
    at = lax.broadcasted_iota(jnp.int32, (count, idx.shape[1]), 0)
    return (at == idx).astype(F32)


VMEM_MIB = 54
PARTS = (8, 8, 6)
MESH = pl.DeviceIdType.MESH


class Sent:
    def __init__(self, src, dst, send_sem, recv_sem, dev, log):
        self.c = pltpu.make_async_remote_copy(src_ref=src, dst_ref=dst, send_sem=send_sem, recv_sem=recv_sem,
                                              device_id=dev, device_id_type=MESH)
        self.c.start()
        self.arrived = False
        log.append(self)

    def wait_recv(self):
        if not self.arrived:
            self.c.wait_recv()
            self.arrived = True

    def close(self):
        self.wait_recv()
        self.c.wait_send()


class Place:
    def __init__(self):
        b, s = lax.axis_index("blk"), lax.axis_index("sub")
        self.blk, self.sub = b, s
        self.core = lax.rem(b, 2)
        self.pos = [b // 4, lax.rem(b // 2, 2) * 2 + lax.rem(s, 2), s // 2]

    def at(self, pos, core):
        return ((pos[0] * 2 + pos[1] // 2) * 2 + core, pos[2] * 2 + lax.rem(pos[1], 2))

    def shift(self, axis, d):
        pos = list(self.pos)
        pos[axis] = lax.rem(pos[axis] + d, 4)
        return self.at(pos, self.core)

    def partition(self, d):
        return (lax.rem(self.blk + d, 16), self.sub)

    def sibling(self):
        return self.at(self.pos, 1 - self.core)


class Reduce:
    def __init__(self, place, n, off, g, full, rba, rbb, s1, rb2, s2, rb3, send_sems, recv_sems):
        self.p, self.n, self.off = place, n, off
        self.g, self.rba, self.rbb, self.s1, self.rb2, self.s2, self.rb3, self.full = g, rba, rbb, s1, rb2, s2, rb3, full
        self.send_sems, self.recv_sems = send_sems, recv_sems

    def put(self, step, part, src, dst, dev):
        pltpu.make_async_remote_copy(src_ref=src, dst_ref=dst, send_sem=self.send_sems.at[int(step == 8), part],
                                     recv_sem=self.recv_sems.at[step, part], device_id=dev,
                                     device_id_type=MESH).start()

    def got(self, step, part, tiles):
        ref = self.full.at[0, pl.ds(0, tiles)]
        pltpu.make_async_copy(ref, ref, self.recv_sems.at[step, part]).wait()

    def close(self):
        for part in range(3):
            for k, tiles in enumerate((33 * self.n, 16 * self.n)):
                ref = self.full.at[0, pl.ds(0, tiles)]
                pltpu.make_async_copy(ref, ref, self.send_sems.at[k, part]).wait()

    def axis(self, part, level):
        return (part + level) % 3

    def here(self, part, level):
        return self.p.pos[self.axis(part, level)]

    def half(self, part, c, k, level=0):
        return pl.ds(self.off + part * 16 * self.n + c * (4 * self.n) + k * (2 * self.n), 2 * self.n)

    def rs1(self, part):
        n, c, a = self.n, self.here(part, 0), self.axis(part, 0)
        for k, d in enumerate((1, 3)):
            self.put(0, part, self.g.at[self.half(part, lax.rem(c + 2, 4), k)], self.rba.at[part, k], self.p.shift(a, d))
        for k, d in enumerate((1, 3)):
            self.put(1, part, self.g.at[self.half(part, lax.rem(c + d, 4), 1 - k)],
                     self.rbb.at[part, k, pl.ds((1 - k) * 2 * n, 2 * n)], self.p.shift(a, d))

    def rs1_mid(self, part):
        n, c, a = self.n, self.here(part, 0), self.axis(part, 0)
        self.got(0, part, 4 * n)
        for k, d in enumerate((1, 3)):
            here = self.half(part, lax.rem(c + d, 4), k)
            self.g[here] = self.g[here] + self.rba[part, k]
            self.put(1, part, self.g.at[here], self.rbb.at[part, k, pl.ds(k * 2 * n, 2 * n)], self.p.shift(a, d))

    def rs1_done(self, part):
        n, c = self.n, self.here(part, 0)
        self.got(1, part, 8 * n)
        off = self.off + part * 16 * n + c * (4 * n)
        self.s1[part] = self.g[pl.ds(off, 4 * n)] + (self.rbb[part, 0] + self.rbb[part, 1])

    def rs2(self, part):
        n, c, a = self.n, self.here(part, 1), self.axis(part, 1)
        for d in (2, 1, 3):
            self.put(2, part, self.s1.at[part, pl.ds(lax.rem(c + d, 4) * n, n)], self.rb2.at[part, d - 1],
                     self.p.shift(a, d))

    def rs2_done(self, part):
        n, c = self.n, self.here(part, 1)
        self.got(2, part, 3 * n)
        self.s2[part] = (self.s1[part, pl.ds(c * n, n)] + self.rb2[part, 0]) + (self.rb2[part, 1] + self.rb2[part, 2])

    def ar3(self, part):
        c, a = self.here(part, 2), self.axis(part, 2)
        for d in (2, 1, 3):
            self.put(3, part, self.s2.at[part], self.rb3.at[part, c], self.p.shift(a, d))
        self.rb3[part, c] = self.s2[part]

    def mine(self, part):
        n = self.n
        return self.off + part * 16 * n + self.here(part, 0) * (4 * n) + self.here(part, 1) * n

    def ar3_done(self, part):
        self.got(3, part, 3 * self.n)
        self.full[self.p.core, pl.ds(self.mine(part), self.n)] = (
            (self.rb3[part, 0] + self.rb3[part, 1]) + (self.rb3[part, 2] + self.rb3[part, 3]))

    def ag2(self, part):
        a = self.axis(part, 1)
        ref = self.full.at[self.p.core, pl.ds(self.mine(part), self.n)]
        for d in (2, 1, 3):
            self.put(4, part, ref, ref, self.p.shift(a, d))

    def ag2_done(self, part):
        self.got(4, part, 3 * self.n)

    def chunk(self, part, c):
        return self.full.at[self.p.core, pl.ds(self.off + part * 16 * self.n + c * (4 * self.n), 4 * self.n)]

    def far(self, part, c, k):
        return self.full.at[self.p.core, self.half(part, c, k)]

    def ag1(self, part):
        c, a = self.here(part, 0), self.axis(part, 0)
        for j in range(2):
            for k, d in enumerate((1, 3)):
                ref = self.far(part, c, (k + j) % 2)
                self.put(5 + j, part, ref, ref, self.p.shift(a, d))
        ref = self.chunk(part, c)
        self.put(8, part, ref, ref, self.p.sibling())

    def ag1_mid(self, part):
        c, a = self.here(part, 0), self.axis(part, 0)
        self.got(5, part, 4 * self.n)
        for k, d in enumerate((1, 3)):
            ref = self.far(part, lax.rem(c + 4 - d, 4), k)
            self.put(7, part, ref, ref, self.p.shift(a, d))

    def ag1_near(self, part):
        c = self.here(part, 0)
        self.got(6, part, 4 * self.n)
        for k, d in enumerate((1, 3)):
            ref = self.chunk(part, lax.rem(c + 4 - d, 4))
            self.put(8, part, ref, ref, self.p.sibling())

    def ag1_done(self, part):
        c = self.here(part, 0)
        self.got(7, part, 4 * self.n)
        ref = self.chunk(part, lax.rem(c + 2, 4))
        self.put(8, part, ref, ref, self.p.sibling())

    def both(self, part):
        self.got(8, part, 16 * self.n)

    def each(self, *steps):
        for part in range(3):
            for step in steps:
                step(part)


def tiles_of(x):
    return [x[:, k : k + 128].reshape(x.shape[0] // 8, 8, 128) for k in range(0, x.shape[1], 128)]


def scatter_into(g_ref, at, grad2, col, base, width, add):
    hot = lanes_hot(col, base, width).astype(F32).astype(BF16)
    for j, t in enumerate(tiles_of(fold(mm(grad2, hot)))):
        n = t.shape[0]
        here = pl.ds(at + j * n, n)
        g_ref[here] = g_ref[here] + t if add else t


def buckets(w, left_ref, lstate_ref, right_ref, rstate_ref, rel_ref, relstate_ref, hub_ref, hstate_ref, heads_hbm, rels_hbm, tails_hbm,
            negs_hbm, hubs_hbm, left_out, right_out, hub_t, rel,
            left, lstate, right, rstate, relstate, hstate, heads, rels, tails, negs, hubs,
            r_buf, dut, dus, dro, drs, mout, min_, g, full, xsem, isem, *batches):
    place = Place()
    log, loads = [], {}
    feats, rows = left.shape
    e = heads.shape[1]
    m = hubs.shape[1]
    for k, (name, src, dst) in enumerate((
            ("rels", rels_hbm, rels), ("heads", heads_hbm, heads), ("rel", rel_ref, rel), ("left", left_ref, left),
            ("right", right_ref, right), ("tails", tails_hbm, tails), ("negs", negs_hbm, negs),
            ("rstate", rstate_ref, rstate), ("lstate", lstate_ref, lstate), ("hubs", hubs_hbm, hubs),
            ("hub", hub_ref, hub_t), ("relstate", relstate_ref, relstate), ("hstate", hstate_ref, hstate))):
        loads[name] = pltpu.make_async_copy(src, dst, isem.at[k])
        if not name.startswith("hub"):
            loads[name].start()
    hub_tiles = feats // 8 * (hub_t.shape[1] // 256)
    rel_tiles = feats // 8 * (rel.shape[1] // 256)
    red, off = [], 0
    for n in PARTS:
        red.append(Reduce(place, n, off, g, full, *batches[8 * len(red) : 8 * len(red) + 8]))
        off += 48 * n
    ha, hb, rc = red
    barrier = pltpu.get_barrier_semaphore()
    for a in range(3):
        for d in (1, 2, 3):
            pl.semaphore_signal(barrier, inc=1, device_id=place.shift(a, d), device_id_type=MESH)
    for dev in (place.sibling(), place.partition(1), place.partition(15)):
        pl.semaphore_signal(barrier, inc=1, device_id=dev, device_id_type=MESH)

    def send(k, src, dst, dev):
        return Sent(src, dst, xsem.at[0, k], xsem.at[1, k], dev, log)

    for name in ("heads", "rels", "left", "rel"):
        loads[name].wait()
    loads["hub"].start()
    loads["hubs"].start()
    idx_r = jnp.concatenate([rels[0:1, :], rels[1:2, :]], axis=1)
    r_buf[...] = fold(mm(stacked(rel[...]), rows_hot(idx_r, 0, rel.shape[1])))
    h0 = fold(gather(left[...], heads[0:1, :]))
    q0 = cmul(h0, r_buf[:, :e])
    for name in ("right", "tails", "negs", "rstate"):
        loads[name].wait()
    q0t = stacked(q0.T)
    q02 = stacked(q0)
    r2 = stacked(right[...])
    coef = coefs(mm3(q0t, r2[:feats], r2[feats:]), w, tails[0:1, :], negs[0:1, :], rows)
    ch, cl = halves(coef)
    mout[:feats, :], state1 = adagrad(right[...], rstate[...], mm3(q02, ch, cl))
    mout[feats:, :] = jnp.broadcast_to(state1, (8, rows))
    pl.semaphore_wait(barrier, 12)
    x_m = send(3, mout, min_, place.partition(1))

    loads["hubs"].wait()
    loads["hub"].wait()
    idx_u = jnp.concatenate([hubs[0:1, :], hubs[1:2, :]], axis=1)
    u = mm(stacked(hub_t[...]), rows_hot(idx_u, 0, hub_t.shape[1])).astype(BF16)
    u0, u1 = u[:, :m], u[:, m:]
    ch2, cl2 = halves(sigmoid(mm3(q0t, u0[:feats], u0[feats:])) * w)
    dq = mm3(r2, ch, cl, NT) + mm3(u0, ch2, cl2, NT)
    dh = cmul_conj(dq, r_buf[:, :e])
    gl = fold(mm(stacked(dh), lanes_hot(column(heads[0:1, :]), 0, rows).astype(F32).astype(BF16)))
    loads["lstate"].wait()
    left[...], lstate[...] = adagrad(left[...], lstate[...], gl)
    h1 = fold(gather(left[...], heads[1:2, :]))
    q1 = cmul(h1, r_buf[:, e:])
    q1t = stacked(q1.T)
    q12 = stacked(q1)
    ch3, cl3 = halves(sigmoid(mm3(q1t, u1[:feats], u1[feats:])) * w)
    dut[:feats, :m] = mm3(q02, ch2, cl2)
    dut[:feats, m:] = mm3(q12, ch3, cl3)
    dut[feats:, :] = jnp.broadcast_to(idx_u.astype(F32), (8, 2 * m))
    x_u = send(0, dut, dus, place.sibling())

    dro[0, :feats, :] = cmul_conj(dq, h0)
    dro[0, feats:, :] = jnp.broadcast_to(rels[0:1, :].astype(F32), (8, e))
    x_r0 = send(1, dro.at[0], drs.at[0], place.sibling())

    half_lanes = hub_t.shape[1] // 2
    first_lane = place.core * half_lanes
    own2 = stacked(dut[:feats, :])
    own_col = column(idx_u)
    for k in range(4):
        scatter_into(g, k * 200, own2, own_col, first_lane + k * 512, 512, False)
    g[hub_tiles + rel_tiles :] = jnp.zeros((g.shape[0] - hub_tiles - rel_tiles, 8, 128), F32)
    x_u.wait_recv()
    sib2 = stacked(dus[:feats, :])
    sib_col = column(dus[feats : feats + 1, :].astype(jnp.int32))
    for k in range(4):
        scatter_into(g, k * 200, sib2, sib_col, first_lane + k * 512, 512, True)
        if k == 1:
            ha.each(ha.rs1)
    hb.each(hb.rs1)

    dq1h = mm3(u1, ch3, cl3, NT)
    first_rel = place.core * (rel.shape[1] // 2)

    def rel_scatter(x, add):
        scatter_into(g, hub_tiles, stacked(x[:feats, :]), column(x[feats : feats + 1, :].astype(jnp.int32)), first_rel, 640,
                     add)

    rel_scatter(dro[0], False)
    x_r0.wait_recv()
    rel_scatter(drs[0], True)
    x_m.wait_recv()
    r2 = stacked(min_[:feats, :])
    score = mm3(q1t, r2[:feats], r2[feats:])
    ha.each(ha.rs1_mid)
    ch, cl = halves(coefs(score, w, tails[1:2, :], negs[1:2, :], rows))
    dq = mm3(r2, ch, cl, NT) + dq1h
    dro[1, :feats, :] = cmul_conj(dq, h1)
    dro[1, feats:, :] = jnp.broadcast_to(rels[1:2, :].astype(F32), (8, e))
    x_r1 = send(2, dro.at[1], drs.at[1], place.sibling())
    hb.each(hb.rs1_mid)
    rel_scatter(dro[1], True)
    x_r1.wait_recv()
    rel_scatter(drs[1], True)
    rc.each(rc.rs1)
    right_out[...], _ = adagrad(min_[:feats, :], min_[feats : feats + 1, :], mm3(q12, ch, cl))
    ha.each(ha.rs1_done, ha.rs2)
    rc.each(rc.rs1_mid)
    hb.each(hb.rs1_done, hb.rs2)
    ha.each(ha.rs2_done, ha.ar3)
    rc.each(rc.rs1_done, rc.rs2)
    hb.each(hb.rs2_done, hb.ar3)
    ha.each(ha.ar3_done, ha.ag2)
    rc.each(rc.rs2_done, rc.ar3)
    hb.each(hb.ar3_done, hb.ag2)
    ha.each(ha.ag2_done, ha.ag1)
    rc.each(rc.ar3_done, rc.ag2)
    hb.each(hb.ag2_done, hb.ag1)
    dh = cmul_conj(dq, r_buf[:, e:])
    gl = fold(mm(stacked(dh), lanes_hot(column(heads[1:2, :]), 0, rows).astype(F32).astype(BF16)))
    left_out[...], _ = adagrad(left[...], lstate[...], gl)
    ha.each(ha.ag1_mid)
    rc.each(rc.ag2_done, rc.ag1)
    ha.each(ha.ag1_near)
    hb.each(hb.ag1_mid)
    rc.each(rc.ag1_mid)
    hb.each(hb.ag1_near)
    ha.each(ha.ag1_done)
    rc.each(rc.ag1_near)
    hb.each(hb.ag1_done)
    loads["hstate"].wait()
    loads["relstate"].wait()

    def final(table, state, first_tile, at, number, lanes):
        n = feats // 8
        count = lanes // 2 // 128
        for h in range(2):
            for j in range(at, at + number):
                here = slice((h * count + j) * 128, (h * count + j + 1) * 128)
                gj = full[h, first_tile + j * n : first_tile + (j + 1) * n].reshape(feats, 128)
                new = state[h * count + j : h * count + j + 1, :] + jnp.sum(gj * gj, axis=0, keepdims=True) * (1.0 / feats)
                table[:, here] = table[:, here] - gj * (RATE / jnp.sqrt(new))

    ha.each(ha.both)
    final(hub_t, hstate, 0, 0, 7, hub_t.shape[1])
    rc.each(rc.ag1_done)
    hb.each(hb.both)
    final(hub_t, hstate, 0, 7, 8, hub_t.shape[1])
    rc.each(rc.both)
    final(hub_t, hstate, 0, 15, 1, hub_t.shape[1])
    final(rel, relstate, hub_tiles, 0, 5, rel.shape[1])
    for c in log + red:
        c.close()


def hand_on(*refs):
    n = (len(refs) - 1) // 2
    copies = []
    for src, dst in zip(refs[:n], refs[n : 2 * n]):
        cut = src.shape[0] // 5
        for k in range(5):
            here = pl.ds(k * cut, cut)
            copies.append(pltpu.make_async_copy(src.at[here], dst.at[here], refs[-1].at[len(copies)]))
            copies[-1].start()
    for c in copies:
        c.wait()


def shards(left_emb, left_state, right_emb, right_state, relation_emb, relation_state, hub_emb, hub_state, heads,
           relations, tails, negatives, hub_ids):
    two, half, rows = left_emb.shape
    feats = two * half
    e = heads.shape[1]
    m = hub_ids.shape[1]
    w = 1.0 / (negatives.shape[1] + hub_ids.shape[1])
    left = left_emb.reshape(feats, rows)
    right = right_emb.reshape(feats, rows)
    rel = relation_emb.reshape(feats, -1)
    hub = hub_emb.reshape(feats, -1)
    sd = lambda *s: jax.ShapeDtypeStruct(s, F32)
    vm = pl.BlockSpec(memory_space=pltpu.VMEM)
    hbm = pl.BlockSpec(memory_space=pl.ANY)
    tile = lambda *s: pltpu.VMEM((*s, 8, 128), F32)
    fl = lambda *s: pltpu.VMEM(s, F32)
    it = lambda *s: pltpu.VMEM(s, jnp.int32)
    dma = pltpu.SemaphoreType.DMA
    batch = lambda n: [tile(3, 2, 2 * n), tile(3, 2, 4 * n), tile(3, 4 * n), tile(3, 3, n), tile(3, n), tile(3, 4, n),
                       dma((2, 3)), dma((9, 3))]
    total = 48 * sum(PARTS)
    outs = [fl(feats, rows), fl(feats, rows), fl(*hub.shape), fl(*rel.shape)]
    left2, right2, hub_new, rel_new = pl.pallas_call(
        functools.partial(buckets, w), out_shape=outs, in_specs=[hbm] * 13, out_specs=[vm] * 4,
        scratch_shapes=[
            fl(feats, rows), fl(1, rows), fl(feats, rows), fl(1, rows),
            fl(rel.shape[1] // 128, 128), fl(hub.shape[1] // 128, 128),
            it(2, e), it(2, e), it(2, e), it(2, negatives.shape[1]), it(2, m),
            fl(feats, 2 * e), fl(feats + 8, 2 * m), fl(feats + 8, 2 * m), fl(2, feats + 8, e), fl(2, feats + 8, e),
            fl(feats + 8, rows), fl(feats + 8, rows), tile(total), tile(2, total),
            dma((2, 4)), dma((13,)), *(x for n in PARTS for x in batch(n))],
        compiler_params=pltpu.CompilerParams(vmem_limit_bytes=VMEM_MIB * 2**20, collective_id=1, has_side_effects=True),
        name="buckets",
    )(left, left_state[None], right, right_state[None], rel, relation_state.reshape(-1, 128), hub,
      hub_state.reshape(-1, 128), heads, relations, tails, negatives, hub_ids)
    outs = [left2, right2, rel_new, hub_new]
    left2, right2, rel_new, hub_new = pl.pallas_call(
        hand_on, out_shape=[sd(*x.shape) for x in outs], in_specs=[vm] * 4, out_specs=[hbm] * 4,
        scratch_shapes=[dma((len(outs) * 5,))], name="hand_on",
        compiler_params=pltpu.CompilerParams(vmem_limit_bytes=4 * 2**20),
    )(*(pltpu.with_memory_space_constraint(x, pltpu.VMEM) for x in outs))
    return (left2.reshape(left_emb.shape), right2.reshape(right_emb.shape), rel_new.reshape(relation_emb.shape),
            hub_new.reshape(hub_emb.shape))


def solution(mesh):
    cut = P(None, None, ("blk", "sub"))
    row = P(("blk", "sub"))
    idx = P(None, ("blk", "sub"))
    return jax.shard_map(shards, mesh=mesh, in_specs=(cut, row, cut, row, P(), P(), P(), P(), idx, idx, idx, idx, idx),
                         out_specs=(cut, cut, P(), P()), check_vma=False)
```

```python
import functools
import jax
import jax.numpy as jnp
from jax import lax
from jax.experimental import pallas as pl
from jax.experimental.pallas import tpu as pltpu
from jax.sharding import PartitionSpec as P

RATE = 0.25
F32, BF16 = jnp.float32, jnp.bfloat16
NN = (((1,), (0,)), ((), ()))
NT = (((1,), (1,)), ((), ()))


def mm(a, b, dims=NN):
    return lax.dot_general(a, b, dims, preferred_element_type=F32)


def halves(x):
    hi = x.astype(BF16)
    return hi, (x - hi.astype(F32)).astype(BF16)


def stacked(x):
    hi, lo = halves(x)
    return jnp.concatenate([hi, lo], axis=0)


def mm3(a2, b_hi, b_lo, dims=NN):
    n = a2.shape[0] // 2
    both = mm(a2, b_hi, dims)
    return both[:n] + both[n:] + mm(a2[:n], b_lo, dims)


def fold(x):
    n = x.shape[0] // 2
    return x[:n] + x[n:]


def rows_hot(idx, base, count):
    at = lax.broadcasted_iota(jnp.int32, (count, idx.shape[1]), 0) + base
    return (at == idx).astype(F32).astype(BF16)


def column(idx):
    parts = []
    for k in range(0, idx.shape[1], 128):
        parts.append(jnp.broadcast_to(idx[:, k : k + 128], (128, 128)).T)
    return jnp.concatenate(parts, axis=0)


def lanes_hot(col, base, count):
    at = lax.broadcasted_iota(jnp.int32, (col.shape[0], 128), 1)
    return jnp.concatenate([col == at + (base + k) for k in range(0, count, 128)], axis=1)


def adagrad(table, state, grad):
    new_state = state + jnp.sum(grad * grad, axis=0, keepdims=True) * (1.0 / grad.shape[0])
    return table - grad * (RATE / jnp.sqrt(new_state)), new_state


def sigmoid(x):
    return 1.0 / (1.0 + jnp.exp(-x))


def cmul(a, b):
    n = a.shape[0] // 2
    a0, a1, b0, b1 = a[:n], a[n:], b[:n], b[n:]
    return jnp.concatenate([a0 * b0 - a1 * b1, a0 * b1 + a1 * b0], axis=0)


def cmul_conj(a, b):
    n = a.shape[0] // 2
    a0, a1, b0, b1 = a[:n], a[n:], b[:n], b[n:]
    return jnp.concatenate([a0 * b0 + a1 * b1, a1 * b0 - a0 * b1], axis=0)


def gather_loop(table_ref, idx, out_ref, block):
    count = table_ref.shape[1]
    out_ref[...] = jnp.zeros_like(out_ref)

    @pl.loop(0, count // block)
    def _(k):
        base = pl.multiple_of(k * block, block)
        out_ref[...] += mm(stacked(table_ref[:, pl.ds(base, block)]), rows_hot(idx, base, block))


def gather(table, idx):
    return mm(stacked(table), rows_hot(idx, 0, table.shape[1]))


def queries_side(q):
    qt = q.T
    return stacked(qt)


def coefs(score, w, tail_idx, neg_idx, rows):
    times = jnp.sum(rows_hot_f(neg_idx, rows), axis=1, keepdims=True)
    times = jnp.broadcast_to(times, (rows, 128)).T[0:1, :] * w
    tail = lanes_hot(column(tail_idx), 0, rows)
    s = sigmoid(score)
    return s * times + jnp.where(tail, s - 1.0, 0.0)


def rows_hot_f(idx, count):
    at = lax.broadcasted_iota(jnp.int32, (count, idx.shape[1]), 0)
    return (at == idx).astype(F32)


VMEM_MIB = 54
PARTS = (8, 8, 6)
MESH = pl.DeviceIdType.MESH


class Sent:
    def __init__(self, src, dst, send_sem, recv_sem, dev, log):
        self.c = pltpu.make_async_remote_copy(src_ref=src, dst_ref=dst, send_sem=send_sem, recv_sem=recv_sem,
                                              device_id=dev, device_id_type=MESH)
        self.c.start()
        self.arrived = False
        log.append(self)

    def wait_recv(self):
        if not self.arrived:
            self.c.wait_recv()
            self.arrived = True

    def close(self):
        self.wait_recv()
        self.c.wait_send()


class Place:
    def __init__(self):
        b, s = lax.axis_index("blk"), lax.axis_index("sub")
        self.blk, self.sub = b, s
        self.core = lax.rem(b, 2)
        self.pos = [b // 4, lax.rem(b // 2, 2) * 2 + lax.rem(s, 2), s // 2]

    def at(self, pos, core):
        return ((pos[0] * 2 + pos[1] // 2) * 2 + core, pos[2] * 2 + lax.rem(pos[1], 2))

    def shift(self, axis, d):
        pos = list(self.pos)
        pos[axis] = lax.rem(pos[axis] + d, 4)
        return self.at(pos, self.core)

    def partition(self, d):
        return (lax.rem(self.blk + d, 16), self.sub)

    def sibling(self):
        return self.at(self.pos, 1 - self.core)


class Reduce:
    def __init__(self, direct, place, n, off, g, full, rba, rbb, s1, rb2, s2, rb3, send_sems, recv_sems):
        self.direct = direct
        self.p, self.n, self.off = place, n, off
        self.g, self.rba, self.rbb, self.s1, self.rb2, self.s2, self.rb3, self.full = g, rba, rbb, s1, rb2, s2, rb3, full
        self.send_sems, self.recv_sems = send_sems, recv_sems

    def put(self, step, part, src, dst, dev):
        pltpu.make_async_remote_copy(src_ref=src, dst_ref=dst, send_sem=self.send_sems.at[int(step == 8), part],
                                     recv_sem=self.recv_sems.at[step, part], device_id=dev,
                                     device_id_type=MESH).start()

    def got(self, step, part, tiles):
        ref = self.full.at[0, pl.ds(0, tiles)]
        pltpu.make_async_copy(ref, ref, self.recv_sems.at[step, part]).wait()

    def close(self):
        for part in range(3):
            for k, tiles in enumerate((33 * self.n, 16 * self.n)):
                ref = self.full.at[0, pl.ds(0, tiles)]
                pltpu.make_async_copy(ref, ref, self.send_sems.at[k, part]).wait()

    def axis(self, part, level):
        return (part + level) % 3

    def here(self, part, level):
        return self.p.pos[self.axis(part, level)]

    def half(self, part, c, k, level=0):
        return pl.ds(self.off + part * 16 * self.n + c * (4 * self.n) + k * (2 * self.n), 2 * self.n)

    def rs1(self, part):
        n, c, a = self.n, self.here(part, 0), self.axis(part, 0)
        for k, d in enumerate((1, 3)):
            self.put(0, part, self.g.at[self.half(part, lax.rem(c + 2, 4), k)], self.rba.at[part, k], self.p.shift(a, d))
        for k, d in enumerate((1, 3)):
            self.put(1, part, self.g.at[self.half(part, lax.rem(c + d, 4), 1 - k)],
                     self.rbb.at[part, k, pl.ds((1 - k) * 2 * n, 2 * n)], self.p.shift(a, d))

    def rs1_mid(self, part):
        n, c, a = self.n, self.here(part, 0), self.axis(part, 0)
        self.got(0, part, 4 * n)
        for k, d in enumerate((1, 3)):
            here = self.half(part, lax.rem(c + d, 4), k)
            self.g[here] = self.g[here] + self.rba[part, k]
            self.put(1, part, self.g.at[here], self.rbb.at[part, k, pl.ds(k * 2 * n, 2 * n)], self.p.shift(a, d))

    def rs1_done(self, part):
        n, c = self.n, self.here(part, 0)
        self.got(1, part, 8 * n)
        off = self.off + part * 16 * n + c * (4 * n)
        self.s1[part] = self.g[pl.ds(off, 4 * n)] + (self.rbb[part, 0] + self.rbb[part, 1])

    def rs2(self, part):
        n, c, a = self.n, self.here(part, 1), self.axis(part, 1)
        for d in (2, 1, 3):
            self.put(2, part, self.s1.at[part, pl.ds(lax.rem(c + d, 4) * n, n)], self.rb2.at[part, d - 1],
                     self.p.shift(a, d))

    def rs2_done(self, part):
        n, c = self.n, self.here(part, 1)
        self.got(2, part, 3 * n)
        self.s2[part] = (self.s1[part, pl.ds(c * n, n)] + self.rb2[part, 0]) + (self.rb2[part, 1] + self.rb2[part, 2])

    def ar3(self, part):
        c, a = self.here(part, 2), self.axis(part, 2)
        for d in (2, 1, 3):
            self.put(3, part, self.s2.at[part], self.rb3.at[part, c], self.p.shift(a, d))
        self.rb3[part, c] = self.s2[part]

    def mine(self, part):
        n = self.n
        return self.off + part * 16 * n + self.here(part, 0) * (4 * n) + self.here(part, 1) * n

    def ar3_done(self, part):
        self.got(3, part, 3 * self.n)
        self.full[self.p.core, pl.ds(self.mine(part), self.n)] = (
            (self.rb3[part, 0] + self.rb3[part, 1]) + (self.rb3[part, 2] + self.rb3[part, 3]))

    def ag2(self, part):
        a = self.axis(part, 1)
        ref = self.full.at[self.p.core, pl.ds(self.mine(part), self.n)]
        for d in (2, 1, 3):
            self.put(4, part, ref, ref, self.p.shift(a, d))

    def ag2_done(self, part):
        self.got(4, part, 3 * self.n)

    def chunk(self, part, c):
        return self.full.at[self.p.core, pl.ds(self.off + part * 16 * self.n + c * (4 * self.n), 4 * self.n)]

    def far(self, part, c, k):
        return self.full.at[self.p.core, self.half(part, c, k)]

    def ag1(self, part):
        c, a = self.here(part, 0), self.axis(part, 0)
        if self.direct:
            ref = self.chunk(part, c)
            for d in (2, 1, 3):
                self.put(5, part, ref, ref, self.p.shift(a, d))
            self.put(8, part, ref, ref, self.p.sibling())
            return
        for j in range(2):
            for k, d in enumerate((1, 3)):
                ref = self.far(part, c, (k + j) % 2)
                self.put(5 + j, part, ref, ref, self.p.shift(a, d))
        ref = self.chunk(part, c)
        self.put(8, part, ref, ref, self.p.sibling())

    def ag1_mid(self, part):
        c, a = self.here(part, 0), self.axis(part, 0)
        self.got(5, part, 4 * self.n)
        for k, d in enumerate((1, 3)):
            ref = self.far(part, lax.rem(c + 4 - d, 4), k)
            self.put(7, part, ref, ref, self.p.shift(a, d))

    def ag1_near(self, part):
        c = self.here(part, 0)
        self.got(6, part, 4 * self.n)
        for k, d in enumerate((1, 3)):
            ref = self.chunk(part, lax.rem(c + 4 - d, 4))
            self.put(8, part, ref, ref, self.p.sibling())

    def ag1_done(self, part):
        c = self.here(part, 0)
        if self.direct:
            self.got(5, part, 12 * self.n)
            for d in (1, 2, 3):
                ref = self.chunk(part, lax.rem(c + d, 4))
                self.put(8, part, ref, ref, self.p.sibling())
            return
        self.got(7, part, 4 * self.n)
        ref = self.chunk(part, lax.rem(c + 2, 4))
        self.put(8, part, ref, ref, self.p.sibling())

    def both(self, part):
        self.got(8, part, 16 * self.n)

    def each(self, *steps):
        for part in range(3):
            for step in steps:
                step(part)


def tiles_of(x):
    return [x[:, k : k + 128].reshape(x.shape[0] // 8, 8, 128) for k in range(0, x.shape[1], 128)]


def scatter_into(g_ref, at, grad2, col, base, width, add):
    hot = lanes_hot(col, base, width).astype(F32).astype(BF16)
    for j, t in enumerate(tiles_of(fold(mm(grad2, hot)))):
        n = t.shape[0]
        here = pl.ds(at + j * n, n)
        g_ref[here] = g_ref[here] + t if add else t


def buckets(w, left_ref, lstate_ref, right_ref, rstate_ref, rel_ref, relstate_ref, hub_ref, hstate_ref, heads_hbm, rels_hbm, tails_hbm,
            negs_hbm, hubs_hbm, left_out, right_out, hub_t, rel,
            left, lstate, right, rstate, relstate, hstate, heads, rels, tails, negs, hubs,
            r_buf, dut, dus, dro, drs, mout, min_, g, full, xsem, isem, *batches):
    place = Place()
    log, loads = [], {}
    feats, rows = left.shape
    e = heads.shape[1]
    m = hubs.shape[1]
    for k, (name, src, dst) in enumerate((
            ("rels", rels_hbm, rels), ("heads", heads_hbm, heads), ("rel", rel_ref, rel), ("left", left_ref, left),
            ("right", right_ref, right), ("tails", tails_hbm, tails), ("negs", negs_hbm, negs),
            ("rstate", rstate_ref, rstate), ("lstate", lstate_ref, lstate), ("hubs", hubs_hbm, hubs),
            ("hub", hub_ref, hub_t), ("relstate", relstate_ref, relstate), ("hstate", hstate_ref, hstate))):
        loads[name] = pltpu.make_async_copy(src, dst, isem.at[k])
        if not name.startswith("hub"):
            loads[name].start()
    hub_tiles = feats // 8 * (hub_t.shape[1] // 256)
    rel_tiles = feats // 8 * (rel.shape[1] // 256)
    red, off = [], 0
    for n in PARTS:
        red.append(Reduce(len(red) == 2, place, n, off, g, full, *batches[8 * len(red) : 8 * len(red) + 8]))
        off += 48 * n
    ha, hb, rc = red
    barrier = pltpu.get_barrier_semaphore()
    for a in range(3):
        for d in (1, 2, 3):
            pl.semaphore_signal(barrier, inc=1, device_id=place.shift(a, d), device_id_type=MESH)
    for dev in (place.sibling(), place.partition(1), place.partition(15)):
        pl.semaphore_signal(barrier, inc=1, device_id=dev, device_id_type=MESH)

    def send(k, src, dst, dev):
        return Sent(src, dst, xsem.at[0, k], xsem.at[1, k], dev, log)

    for name in ("heads", "rels", "left", "rel"):
        loads[name].wait()
    loads["hub"].start()
    loads["hubs"].start()
    idx_r = jnp.concatenate([rels[0:1, :], rels[1:2, :]], axis=1)
    r_buf[...] = fold(mm(stacked(rel[...]), rows_hot(idx_r, 0, rel.shape[1])))
    h0 = fold(gather(left[...], heads[0:1, :]))
    q0 = cmul(h0, r_buf[:, :e])
    for name in ("right", "tails", "negs", "rstate"):
        loads[name].wait()
    q0t = stacked(q0.T)
    q02 = stacked(q0)
    r2 = stacked(right[...])
    coef = coefs(mm3(q0t, r2[:feats], r2[feats:]), w, tails[0:1, :], negs[0:1, :], rows)
    ch, cl = halves(coef)
    mout[:feats, :], state1 = adagrad(right[...], rstate[...], mm3(q02, ch, cl))
    mout[feats:, :] = jnp.broadcast_to(state1, (8, rows))
    pl.semaphore_wait(barrier, 12)
    x_m = send(3, mout, min_, place.partition(1))

    loads["hubs"].wait()
    loads["hub"].wait()
    idx_u = jnp.concatenate([hubs[0:1, :], hubs[1:2, :]], axis=1)
    u = mm(stacked(hub_t[...]), rows_hot(idx_u, 0, hub_t.shape[1])).astype(BF16)
    u0, u1 = u[:, :m], u[:, m:]
    ch2, cl2 = halves(sigmoid(mm3(q0t, u0[:feats], u0[feats:])) * w)
    dq = mm3(r2, ch, cl, NT) + mm3(u0, ch2, cl2, NT)
    dh = cmul_conj(dq, r_buf[:, :e])
    gl = fold(mm(stacked(dh), lanes_hot(column(heads[0:1, :]), 0, rows).astype(F32).astype(BF16)))
    loads["lstate"].wait()
    left[...], lstate[...] = adagrad(left[...], lstate[...], gl)
    h1 = fold(gather(left[...], heads[1:2, :]))
    q1 = cmul(h1, r_buf[:, e:])
    q1t = stacked(q1.T)
    q12 = stacked(q1)
    ch3, cl3 = halves(sigmoid(mm3(q1t, u1[:feats], u1[feats:])) * w)
    dut[:feats, :m] = mm3(q02, ch2, cl2)
    dut[:feats, m:] = mm3(q12, ch3, cl3)
    dut[feats:, :] = jnp.broadcast_to(idx_u.astype(F32), (8, 2 * m))
    x_u = send(0, dut, dus, place.sibling())

    dro[0, :feats, :] = cmul_conj(dq, h0)
    dro[0, feats:, :] = jnp.broadcast_to(rels[0:1, :].astype(F32), (8, e))
    x_r0 = send(1, dro.at[0], drs.at[0], place.sibling())

    half_lanes = hub_t.shape[1] // 2
    first_lane = place.core * half_lanes
    own2 = stacked(dut[:feats, :])
    own_col = column(idx_u)
    for k in range(4):
        scatter_into(g, k * 200, own2, own_col, first_lane + k * 512, 512, False)
    g[hub_tiles + rel_tiles :] = jnp.zeros((g.shape[0] - hub_tiles - rel_tiles, 8, 128), F32)
    x_u.wait_recv()
    sib2 = stacked(dus[:feats, :])
    sib_col = column(dus[feats : feats + 1, :].astype(jnp.int32))
    for k in range(4):
        scatter_into(g, k * 200, sib2, sib_col, first_lane + k * 512, 512, True)
        if k == 1:
            ha.each(ha.rs1)
    hb.each(hb.rs1)

    dq1h = mm3(u1, ch3, cl3, NT)
    first_rel = place.core * (rel.shape[1] // 2)

    def rel_scatter(x, add):
        scatter_into(g, hub_tiles, stacked(x[:feats, :]), column(x[feats : feats + 1, :].astype(jnp.int32)), first_rel, 640,
                     add)

    rel_scatter(dro[0], False)
    x_r0.wait_recv()
    rel_scatter(drs[0], True)
    x_m.wait_recv()
    r2 = stacked(min_[:feats, :])
    score = mm3(q1t, r2[:feats], r2[feats:])
    ha.each(ha.rs1_mid)
    ch, cl = halves(coefs(score, w, tails[1:2, :], negs[1:2, :], rows))
    dq = mm3(r2, ch, cl, NT) + dq1h
    dro[1, :feats, :] = cmul_conj(dq, h1)
    dro[1, feats:, :] = jnp.broadcast_to(rels[1:2, :].astype(F32), (8, e))
    x_r1 = send(2, dro.at[1], drs.at[1], place.sibling())
    hb.each(hb.rs1_mid)
    rel_scatter(dro[1], True)
    x_r1.wait_recv()
    rel_scatter(drs[1], True)
    rc.each(rc.rs1)
    right_out[...], _ = adagrad(min_[:feats, :], min_[feats : feats + 1, :], mm3(q12, ch, cl))
    ha.each(ha.rs1_done, ha.rs2)
    rc.each(rc.rs1_mid)
    hb.each(hb.rs1_done, hb.rs2)
    ha.each(ha.rs2_done, ha.ar3)
    rc.each(rc.rs1_done, rc.rs2)
    hb.each(hb.rs2_done, hb.ar3)
    ha.each(ha.ar3_done, ha.ag2)
    rc.each(rc.rs2_done, rc.ar3)
    hb.each(hb.ar3_done, hb.ag2)
    ha.each(ha.ag2_done, ha.ag1)
    rc.each(rc.ar3_done, rc.ag2)
    hb.each(hb.ag2_done, hb.ag1)
    dh = cmul_conj(dq, r_buf[:, e:])
    gl = fold(mm(stacked(dh), lanes_hot(column(heads[1:2, :]), 0, rows).astype(F32).astype(BF16)))
    left_out[...], _ = adagrad(left[...], lstate[...], gl)
    ha.each(ha.ag1_mid)
    rc.each(rc.ag2_done, rc.ag1)
    ha.each(ha.ag1_near)
    hb.each(hb.ag1_mid)
    hb.each(hb.ag1_near)
    ha.each(ha.ag1_done)
    hb.each(hb.ag1_done)
    loads["hstate"].wait()
    loads["relstate"].wait()

    def final(table, state, first_tile, at, number, lanes):
        n = feats // 8
        count = lanes // 2 // 128
        for h in range(2):
            for j in range(at, at + number):
                here = slice((h * count + j) * 128, (h * count + j + 1) * 128)
                gj = full[h, first_tile + j * n : first_tile + (j + 1) * n].reshape(feats, 128)
                new = state[h * count + j : h * count + j + 1, :] + jnp.sum(gj * gj, axis=0, keepdims=True) * (1.0 / feats)
                table[:, here] = table[:, here] - gj * (RATE / jnp.sqrt(new))

    ha.each(ha.both)
    final(hub_t, hstate, 0, 0, 7, hub_t.shape[1])
    rc.each(rc.ag1_done)
    hb.each(hb.both)
    final(hub_t, hstate, 0, 7, 8, hub_t.shape[1])
    rc.each(rc.both)
    final(hub_t, hstate, 0, 15, 1, hub_t.shape[1])
    final(rel, relstate, hub_tiles, 0, 5, rel.shape[1])
    for c in log + red:
        c.close()


def hand_on(*refs):
    n = (len(refs) - 1) // 2
    copies = []
    for src, dst in zip(refs[:n], refs[n : 2 * n]):
        cut = src.shape[0] // 5
        for k in range(5):
            here = pl.ds(k * cut, cut)
            copies.append(pltpu.make_async_copy(src.at[here], dst.at[here], refs[-1].at[len(copies)]))
            copies[-1].start()
    for c in copies:
        c.wait()


def shards(left_emb, left_state, right_emb, right_state, relation_emb, relation_state, hub_emb, hub_state, heads,
           relations, tails, negatives, hub_ids):
    two, half, rows = left_emb.shape
    feats = two * half
    e = heads.shape[1]
    m = hub_ids.shape[1]
    w = 1.0 / (negatives.shape[1] + hub_ids.shape[1])
    left = left_emb.reshape(feats, rows)
    right = right_emb.reshape(feats, rows)
    rel = relation_emb.reshape(feats, -1)
    hub = hub_emb.reshape(feats, -1)
    sd = lambda *s: jax.ShapeDtypeStruct(s, F32)
    vm = pl.BlockSpec(memory_space=pltpu.VMEM)
    hbm = pl.BlockSpec(memory_space=pl.ANY)
    tile = lambda *s: pltpu.VMEM((*s, 8, 128), F32)
    fl = lambda *s: pltpu.VMEM(s, F32)
    it = lambda *s: pltpu.VMEM(s, jnp.int32)
    dma = pltpu.SemaphoreType.DMA
    batch = lambda n: [tile(3, 2, 2 * n), tile(3, 2, 4 * n), tile(3, 4 * n), tile(3, 3, n), tile(3, n), tile(3, 4, n),
                       dma((2, 3)), dma((9, 3))]
    total = 48 * sum(PARTS)
    outs = [fl(feats, rows), fl(feats, rows), fl(*hub.shape), fl(*rel.shape)]
    left2, right2, hub_new, rel_new = pl.pallas_call(
        functools.partial(buckets, w), out_shape=outs, in_specs=[hbm] * 13, out_specs=[vm] * 4,
        scratch_shapes=[
            fl(feats, rows), fl(1, rows), fl(feats, rows), fl(1, rows),
            fl(rel.shape[1] // 128, 128), fl(hub.shape[1] // 128, 128),
            it(2, e), it(2, e), it(2, e), it(2, negatives.shape[1]), it(2, m),
            fl(feats, 2 * e), fl(feats + 8, 2 * m), fl(feats + 8, 2 * m), fl(2, feats + 8, e), fl(2, feats + 8, e),
            fl(feats + 8, rows), fl(feats + 8, rows), tile(total), tile(2, total),
            dma((2, 4)), dma((13,)), *(x for n in PARTS for x in batch(n))],
        compiler_params=pltpu.CompilerParams(vmem_limit_bytes=VMEM_MIB * 2**20, collective_id=1, has_side_effects=True),
        name="buckets",
    )(left, left_state[None], right, right_state[None], rel, relation_state.reshape(-1, 128), hub,
      hub_state.reshape(-1, 128), heads, relations, tails, negatives, hub_ids)
    outs = [left2, right2, rel_new, hub_new]
    left2, right2, rel_new, hub_new = pl.pallas_call(
        hand_on, out_shape=[sd(*x.shape) for x in outs], in_specs=[vm] * 4, out_specs=[hbm] * 4,
        scratch_shapes=[dma((len(outs) * 5,))], name="hand_on",
        compiler_params=pltpu.CompilerParams(vmem_limit_bytes=4 * 2**20),
    )(*(pltpu.with_memory_space_constraint(x, pltpu.VMEM) for x in outs))
    return (left2.reshape(left_emb.shape), right2.reshape(right_emb.shape), rel_new.reshape(relation_emb.shape),
            hub_new.reshape(hub_emb.shape))


def solution(mesh):
    cut = P(None, None, ("blk", "sub"))
    row = P(("blk", "sub"))
    idx = P(None, ("blk", "sub"))
    return jax.shard_map(shards, mesh=mesh, in_specs=(cut, row, cut, row, P(), P(), P(), P(), idx, idx, idx, idx, idx),
                         out_specs=(cut, cut, P(), P()), check_vma=False)
```
